128 devices in a mesh: frame: 64 (over z, y, x), tile: 2 (over core).
Axes of the slice: x: 4, y: 4, z: 4, core: 2. Of those that a mesh axis runs over, the one named last changes fastest.
Arguments:
- frames_in: bfloat16 [768, 256, 1152], P('frame', 'tile'), may hold values from -10 to 10
- norm_gain: float32 [1152], replicated, may hold values from 0.5 to 1.5
- norm_bias: float32 [1152], replicated, may hold values from -3 to 3
- w_qkv: bfloat16 [1152, 3456], replicated, may hold values from -3.5 to 3.5
- w_out: bfloat16 [1152, 1152], replicated, may hold values from -0.1875 to 0.1875
- time_taps: float32 [3, 1152], replicated, may hold values from 0.25 to 1
- w_proj: bfloat16 [1152, 3584], P(None, 'tile'), may hold values from -0.1875 to 0.1875
- clip_lengths: int32 [6], replicated, may hold values from 1 to 96, 384 in all
- frame_slot: int32 [768], replicated, may hold values from -1 to 383, as said below
- block_map: int32 [64], replicated, may hold values from 0 to 63, each once
Outputs:
- video_tokens: bfloat16 [384, 64, 3584], P('frame', None, 'tile')
The draws below stay inside these ranges and needn't reach their ends.
Inputs may be any that keep to these rules, and one draw needn't show every extreme that they name: `frame_slot`: each frame 0 to 383 is held by exactly one slot; -1 marks an empty slot; a device's live slots come first among its 12, and some device has all 12 live. `clip_lengths`: the lengths sum to 384; clip 0's frames come first in frame order, then clip 1's, and so on. `block_map`: A permutation.
All inputs are finite; a program needn't handle non-finite values.
Results may differ from the reference program's by a relative error of at most 0.012.
Values may be sent and summed in bfloat16 or wider, within the bound.
No kernel may reach another device: no remote copies, remote signals or barrier semaphores. Data moves between devices by JAX's collectives and lax.ppermute only.
A program may use at most 192 MiB of HBM per device.

```python
import math
import jax
import jax.numpy as jnp
import numpy as np
from jax import lax

D = 1152
HEADS = 16
HEAD_DIM = 72
PATCH = 256
OUT = 3584
CLIPS = 6
FR_DEV = 6
SLOT_DEV = 12
TOTAL_FRAMES = 384
SLOTS_ALL = 768
CLIP_MOST = 96
BLOCKS = 64


def draw_frames_in(key, part):
    key = jax.random.fold_in(key, 11)
    key_base = jax.random.fold_in(key, 0)
    shape_all = (SLOTS_ALL, PATCH, D)
    base_draw = jax.random.normal(key_base, shape_all, jnp.float32)
    return base_draw.astype(jnp.bfloat16)


def draw_w_qkv(key, part):
    key = jax.random.fold_in(key, 23)
    key_base = jax.random.fold_in(key, 0)
    result = jax.random.normal(key_base, (D, 3 * D), jnp.float32) / math.sqrt(D)
    return jnp.clip(result, -3.5, 3.5).astype(jnp.bfloat16)


def draw_frame_slot(key, part):
    key = jax.random.fold_in(key, 37)
    key_surplus, key_order, key_shuffle = jax.random.split(key, 3)
    devices = SLOTS_ALL // SLOT_DEV
    pair_count = devices // 2
    surplus = jax.random.randint(key_surplus, (pair_count,), 0, FR_DEV + 1).astype(jnp.int32)
    surplus = surplus.at[0].set(FR_DEV)
    pair_counts = jnp.stack([FR_DEV + surplus, FR_DEV - surplus], 1).reshape(devices)
    device_order = jax.random.permutation(key_order, devices)
    counts = jnp.zeros((devices,), jnp.int32).at[device_order].set(pair_counts)
    live_slot = jnp.arange(SLOT_DEV, dtype=jnp.int32)[None, :] < counts[:, None]
    live_flat = live_slot.reshape(-1).astype(jnp.int32)
    live_rank = jnp.cumsum(live_flat).astype(jnp.int32) - 1
    shuffled = jax.random.permutation(key_shuffle, TOTAL_FRAMES).astype(jnp.int32)
    slot_frame = jnp.take(shuffled, jnp.clip(live_rank, 0, TOTAL_FRAMES - 1))
    return jnp.where(live_flat == 1, slot_frame, -1).astype(jnp.int32)


def shard_levels(rng, shape, cuts, smallest, top_value):
    factor_of, own = 1.0, jax.random.fold_in(rng, 6)
    for position, shards_of in cuts:
        draws = jnp.exp(jax.random.uniform(jax.random.fold_in(own, position), (shards_of,), jnp.float32, smallest / len(cuts), top_value / len(cuts)))
        factor_of = factor_of * jnp.repeat(draws, shape[position] // shards_of).reshape([-1 if axis == position else 1 for axis in range(len(shape))])
    return factor_of


def length_profile(amount, total, limit, slope):
    loads = [(1 << 20) // math.isqrt(standing ** slope) + 1 for standing in range(2, amount + 1)]
    rest, given = total - limit - (amount - 1), [1] * (amount - 1)
    while rest > 0:
        candidates = [i for i in range(amount - 1) if given[i] < limit]
        pool, budget = sum([loads[i] for i in candidates]), rest
        for i in candidates:
            addition = min(limit - given[i], max(1, budget * loads[i] // pool), rest)
            given[i] = given[i] + addition
            rest = rest - addition
    return np.array([limit] + given)


def uneven_parts(stream_key, count, total, most, lean):
    if count == 2:
        one = jax.random.randint(stream_key, (), max(1, total - most), min(most, total - 1) + 1)
        return jnp.stack([one, total - one])
    tallies = jnp.asarray(length_profile(count, total, most, lean), jnp.int32)
    couples = (count - 1) // 2
    giver, taker = tallies[1:1 + 2 * couples:2], tallies[2:2 + 2 * couples:2]
    slack = jnp.minimum(giver - 1, most - taker)
    moved = jax.random.randint(jax.random.fold_in(stream_key, 1), (couples,), 0, 1 << 20) % (slack + 1)
    tallies = tallies.at[1:1 + 2 * couples:2].set(giver - moved).at[2:2 + 2 * couples:2].set(taker + moved)
    return tallies[jax.random.permutation(jax.random.fold_in(stream_key, 2), count)]


def noise(stream_key, shape, width, reach, shards=(), kind=jnp.bfloat16):
    drawn = width * jax.random.normal(stream_key, shape, jnp.float32)
    if shards:
        drawn = drawn * shard_levels(stream_key, shape, shards, -0.22, 0.18)
    return jnp.clip(drawn, -reach, reach).astype(kind)


def setup_inputs(seed: int = 0) -> dict:
    key_of = jax.random.split(jax.random.key(seed), 11)
    frames_in = draw_frames_in(jax.random.fold_in(key_of[10], 71), 0)
    norm_gain = jnp.clip(1.0 + 0.1 * jax.random.normal(key_of[1], (D,), jnp.float32), 0.5, 1.5)
    norm_bias = noise(key_of[2], (D,), 0.5, 3.0, (), jnp.float32)
    w_qkv = draw_w_qkv(jax.random.fold_in(key_of[10], 71), 0)
    w_out = noise(key_of[4], (D, D), D ** -0.5, 0.1875)
    time_taps = jnp.clip(jax.random.uniform(key_of[5], (3, D), jnp.float32, 0.25, 1.0), 0.25, 1.0)
    w_proj = noise(key_of[6], (D, OUT), D ** -0.5, 0.1875, ((1, 2),))
    clip_lengths = uneven_parts(key_of[7], CLIPS, TOTAL_FRAMES, CLIP_MOST, 1).astype(jnp.int32)
    frame_slot = draw_frame_slot(jax.random.fold_in(key_of[10], 71), 0)
    block_map = jax.random.permutation(key_of[9], BLOCKS).astype(jnp.int32)
    return dict(frames_in=frames_in, norm_gain=norm_gain, norm_bias=norm_bias, w_qkv=w_qkv, w_out=w_out, time_taps=time_taps, w_proj=w_proj, clip_lengths=clip_lengths, frame_slot=frame_slot, block_map=block_map)


norm_eps = 1e-06

def layer_norm(rows_in, norm_gain, norm_bias):
    widened = rows_in.astype(jnp.float32)
    row_mean = lax.optimization_barrier(jnp.mean(widened, -1, keepdims=True))
    centred = widened - row_mean
    variance = lax.optimization_barrier(jnp.mean(centred * centred, -1, keepdims=True))
    return (centred * lax.rsqrt(variance + norm_eps) * norm_gain + norm_bias).astype(jnp.bfloat16)

def encode_frame(one_frame, norm_gain, norm_bias, w_qkv, w_out):
    model_width = one_frame.shape[-1]
    normed = layer_norm(one_frame, norm_gain, norm_bias)
    projected_qkv = jnp.dot(normed, w_qkv, preferred_element_type=jnp.float32).astype(jnp.bfloat16)
    queries = projected_qkv[:, :model_width].reshape(PATCH, HEADS, HEAD_DIM).astype(jnp.float32)
    key_rows = projected_qkv[:, model_width:2 * model_width].reshape(PATCH, HEADS, HEAD_DIM).astype(jnp.float32)
    values = projected_qkv[:, 2 * model_width:].reshape(PATCH, HEADS, HEAD_DIM).astype(jnp.float32)
    scores = jnp.einsum('phd,khd->hpk', queries, key_rows, precision=lax.Precision.HIGHEST) / math.sqrt(HEAD_DIM)
    attention = jax.nn.softmax(scores, -1).astype(jnp.bfloat16)
    context = jnp.einsum('hpk,khd->phd', attention.astype(jnp.float32), values, precision=lax.Precision.HIGHEST)
    context = context.astype(jnp.bfloat16).reshape(PATCH, model_width)
    layer_out = (one_frame.astype(jnp.float32) + jnp.dot(context, w_out, preferred_element_type=jnp.float32)).astype(jnp.bfloat16)
    return lax.optimization_barrier(jnp.mean(layer_out.reshape(PATCH // 4, 4, model_width).astype(jnp.float32), 1)).astype(jnp.bfloat16)

def neighbour_masks(clip_lengths, frame_total):
    starts = (jnp.cumsum(clip_lengths) - clip_lengths).astype(jnp.int32)
    frame_ids = jnp.arange(frame_total, dtype=jnp.int32)
    is_start = jnp.any(frame_ids[:, None] == starts[None, :], 1)
    after_start = jnp.concatenate([is_start[1:], jnp.ones((1,), bool)])
    prev_mask = jnp.where(is_start, 0.0, 1.0).astype(jnp.float32)
    next_mask = jnp.where(after_start, 0.0, 1.0).astype(jnp.float32)
    return (prev_mask, next_mask)

def reference(frames_in, norm_gain, norm_bias, w_qkv, w_out, time_taps, w_proj, clip_lengths, frame_slot, block_map):
    frame_total = TOTAL_FRAMES
    positions = jnp.arange(frame_slot.shape[0], dtype=jnp.int32)
    target = jnp.where(frame_slot >= 0, frame_slot, frame_total).astype(jnp.int32)
    slot_of = jnp.zeros((frame_total,), jnp.int32).at[target].set(positions, mode='drop')
    ordered = jnp.take(frames_in, slot_of, axis=0)
    pooled = lax.map(lambda one_frame: encode_frame(one_frame, norm_gain, norm_bias, w_qkv, w_out), ordered)
    prev_mask, next_mask = neighbour_masks(clip_lengths, frame_total)
    current = pooled.astype(jnp.float32)
    zero_rim = jnp.zeros_like(current[:1])
    earlier = jnp.concatenate([zero_rim, current[:-1]], 0)
    later = jnp.concatenate([current[1:], zero_rim], 0)
    mixed_rows = (time_taps[0] * earlier * prev_mask[:, None, None] + time_taps[1] * current + time_taps[2] * later * next_mask[:, None, None]).astype(jnp.bfloat16)
    projected = jnp.dot(mixed_rows.reshape(-1, mixed_rows.shape[-1]), w_proj, preferred_element_type=jnp.float32)
    projected = projected.astype(jnp.bfloat16).reshape(frame_total, BLOCKS, OUT)
    return jnp.zeros_like(projected).at[:, block_map].set(projected)
```

```python
import math

import jax
import jax.numpy as jnp
from jax import lax
from jax.experimental import pallas as pl
from jax.experimental.pallas import tpu as pltpu
from jax.sharding import PartitionSpec as P

D = 1152
HEADS = 16
HEAD_DIM = 72
PATCH = 256
HALF = 128
BLOCKS = 64
FRAMES = 384
FRAME_DEVS = 64
CLIPS = 6
FR_DEV = 6
SLOT_DEV = 12
PAIRS = 3
OUT_DEV = 1792
NORM_EPS = 1e-6
SCORE_SCALE = math.log2(math.e) / math.sqrt(HEAD_DIM)
VMEM_LIMIT = 56 << 20

bf16 = jnp.bfloat16
f32 = jnp.float32
NT = (((1,), (1,)), ((), ()))


def resident(shape):
    return pl.BlockSpec(shape, lambda *_: (0,) * len(shape), pipeline_mode=pl.Buffered(1))


def head_lanes(head):
    first, last = HEAD_DIM * head, HEAD_DIM * (head + 1) - 1
    return first // 128 * 128, (last // 128 + 1) * 128


def encode_kernel(
    half_ref, own_ref, other_ref, gain_ref, bias_ref, wqkv_ref, wout_ref, place_ref, out_ref,
    x_s, normed_s, qk_s, vt_s, ctx_s,
):
    for s in range(2):
        x_s[s * PATCH : s * PATCH + HALF, :] = own_ref[s]
        x_s[s * PATCH + HALF : (s + 1) * PATCH, :] = other_ref[s]
    for r in range(0, 2 * PATCH, HALF):
        rows = x_s[r : r + HALF, :].astype(f32)
        centred = rows - jnp.sum(rows, -1, keepdims=True) * (1.0 / D)
        variance = jnp.sum(centred * centred, -1, keepdims=True) * (1.0 / D)
        normed = centred * lax.rsqrt(variance + NORM_EPS) * gain_ref[...] + bias_ref[...]
        normed_s[r : r + HALF, :] = normed.astype(bf16)
    for c in range(0, 2 * D, 256):
        part = jnp.dot(normed_s[...], wqkv_ref[:, c : c + 256], preferred_element_type=f32)
        qk_s[:, c : c + 256] = part.astype(bf16)
    for c in range(0, D, 128):
        first = 2 * D + c
        part = jnp.dot(normed_s[...], wqkv_ref[:, first : first + 128], preferred_element_type=f32)
        vt_s[c : c + 128, :] = part.T
    lane = lax.broadcasted_iota(jnp.int32, (1, D), 1)
    ones = jnp.ones((8, PATCH), f32)
    for s in range(2):
        rows = slice(s * PATCH, (s + 1) * PATCH)
        for head in range(HEADS):
            lo, hi = head_lanes(head)
            start = HEAD_DIM * head
            mine = (lane[:, lo:hi] >= start) & (lane[:, lo:hi] < start + HEAD_DIM)
            keys = qk_s[rows, D + lo : D + hi]
            keys = jnp.where(mine, keys, jnp.zeros_like(keys))
            scores = lax.dot_general(keys, qk_s[rows, lo:hi], NT, preferred_element_type=f32)
            top = jnp.max(scores, 0, keepdims=True)
            weights = jnp.exp2((scores - top) * SCORE_SCALE).astype(bf16)
            values = jnp.concatenate([vt_s[start : start + HEAD_DIM, rows], ones], 0).astype(bf16)
            summed = jnp.dot(values, weights, preferred_element_type=f32)
            ctx_s[start : start + HEAD_DIM, rows] = summed[:HEAD_DIM] / summed[HEAD_DIM : HEAD_DIM + 1]
    row = lax.broadcasted_iota(jnp.int32, (2 * BLOCKS, 2 * PATCH), 0)
    col = lax.broadcasted_iota(jnp.int32, (2 * BLOCKS, 2 * PATCH), 1)
    member = (row // 2 == place_ref[...]) & (row % 2 == col // PATCH)
    pool = jnp.where(member, 0.25, 0.0).astype(bf16)
    pooled_ctx = lax.dot_general(pool, ctx_s[...].astype(bf16), NT, preferred_element_type=f32)
    total = jnp.dot(pool, x_s[...], preferred_element_type=f32)
    total += jnp.dot(pooled_ctx.astype(bf16), wout_ref[...], preferred_element_type=f32)
    out_ref[...] = total.astype(bf16).reshape(BLOCKS, 2, D)


def encode(half, frames_in, other, gain, bias, w_qkv, w_out, place):
    return pl.pallas_call(
        encode_kernel,
        grid_spec=pltpu.PrefetchScalarGridSpec(
            num_scalar_prefetch=1,
            grid=(PAIRS,),
            in_specs=[
                pl.BlockSpec((2, HALF, D), lambda i, half: (half[0] * PAIRS + i, 0, 0)),
                pl.BlockSpec((2, HALF, D), lambda i, half: (i, 0, 0)),
                resident((1, D)),
                resident((1, D)),
                resident((D, 3 * D)),
                resident((D, D)),
                resident((1, 2 * PATCH)),
            ],
            out_specs=pl.BlockSpec((BLOCKS, 2, D), lambda i, half: (0, 0, i)),
            scratch_shapes=[
                pltpu.VMEM((2 * PATCH, D), bf16),
                pltpu.VMEM((2 * PATCH, D), bf16),
                pltpu.VMEM((2 * PATCH, 2 * D), bf16),
                pltpu.VMEM((D, 2 * PATCH), f32),
                pltpu.VMEM((D, 2 * PATCH), f32),
            ],
        ),
        out_shape=jax.ShapeDtypeStruct((BLOCKS, 2, PAIRS * D), bf16),
        compiler_params=pltpu.CompilerParams(vmem_limit_bytes=VMEM_LIMIT),
        name="encode_frames",
    )(half, frames_in, other, gain, bias, w_qkv, w_out, place)


def mix_kernel(lengths_ref, held_ref, own_ref, other_ref, taps_ref, out_ref, rows_s):
    step = pl.program_id(0)

    @pl.when(step == 0)
    def _():
        for j in range(PAIRS):
            cols = slice(j * D, (j + 1) * D)
            rows_s[j * 128 : (j + 1) * 128, :] = own_ref[:, :, cols].reshape(128, D)
            rows_s[(j + 3) * 128 : (j + 4) * 128, :] = other_ref[:, :, cols].reshape(128, D)

    row = lax.broadcasted_iota(jnp.int32, (128, 1), 0)
    frame = FR_DEV * (row // 2) + 2 * step + row % 2
    first, last = frame < 0, frame + 1 == FRAMES
    start = 0
    for c in range(CLIPS):
        first |= frame == start
        last |= frame + 1 == start
        start += lengths_ref[c]
    held = held_ref[...]

    def pick(wanted):
        hit = jnp.where(held == wanted, 1.0, 0.0).astype(bf16)
        return jnp.dot(hit, rows_s[...], preferred_element_type=f32)

    earlier = pick(jnp.where(first, -2, frame - 1))
    later = pick(jnp.where(last, -2, frame + 1))
    mixed = taps_ref[0:1] * earlier + taps_ref[1:2] * pick(frame) + taps_ref[2:3] * later
    out_ref[...] = mixed.astype(bf16).reshape(FRAME_DEVS, 2, D)


def mix(lengths, held, own, other, taps):
    return pl.pallas_call(
        mix_kernel,
        grid=(PAIRS,),
        in_specs=[
            pl.BlockSpec(memory_space=pltpu.SMEM),
            resident((1, 768)),
            resident((FRAME_DEVS, 2, PAIRS * D)),
            resident((FRAME_DEVS, 2, PAIRS * D)),
            resident((3, D)),
        ],
        out_specs=pl.BlockSpec((FRAME_DEVS, 2, D), lambda i: (0, 0, i)),
        out_shape=jax.ShapeDtypeStruct((FRAME_DEVS, 2, PAIRS * D), bf16),
        scratch_shapes=[pltpu.VMEM((768, D), bf16)],
        compiler_params=pltpu.CompilerParams(vmem_limit_bytes=VMEM_LIMIT),
        name="mix_rows",
    )(lengths, held, own, other, taps)


def project_kernel(mixed_ref, w_ref, out_ref):
    row = lax.broadcasted_iota(jnp.int32, (128, 128), 0)
    col = lax.broadcasted_iota(jnp.int32, (128, 128), 1)
    swap = jnp.where(col == 2 * (row % BLOCKS) + row // BLOCKS, 1.0, 0.0).astype(bf16)
    rows = mixed_ref[...].reshape(128, D)
    rows = jnp.dot(swap, rows, preferred_element_type=f32).astype(bf16)
    out = jnp.dot(rows, w_ref[...], preferred_element_type=f32).astype(bf16)
    out_ref[...] = out.reshape(2, BLOCKS, OUT_DEV)


def project(mixed, w_proj):
    return pl.pallas_call(
        project_kernel,
        grid=(PAIRS,),
        in_specs=[
            pl.BlockSpec((BLOCKS, 2, D), lambda i: (0, 0, i)),
            resident((D, OUT_DEV)),
        ],
        out_specs=pl.BlockSpec((2, BLOCKS, OUT_DEV), lambda i: (i, 0, 0)),
        out_shape=jax.ShapeDtypeStruct((FR_DEV, BLOCKS, OUT_DEV), bf16),
        compiler_params=pltpu.CompilerParams(vmem_limit_bytes=VMEM_LIMIT),
        name="project_rows",
    )(mixed, w_proj)


SWAP = [(0, 1), (1, 0)]


def on_device(
    frames_in, norm_gain, norm_bias, w_qkv, w_out, time_taps, w_proj, clip_lengths, frame_slot, block_map
):
    tile = lax.axis_index("tile")
    sent = lax.dynamic_slice_in_dim(frames_in, FR_DEV * (1 - tile), FR_DEV)
    other = lax.ppermute(sent, "tile", SWAP)
    halves = block_map.reshape(2, BLOCKS // 2)
    place = jnp.where(tile == 0, halves, halves[::-1]).reshape(BLOCKS)
    place = jnp.tile(jnp.repeat(place, 4), 2)[None]
    half = jnp.reshape(tile, (1,)).astype(jnp.int32)
    pooled = encode(
        half, frames_in, other, norm_gain[None], norm_bias[None], w_qkv, w_out, place
    )
    spread = lax.all_to_all(pooled, "frame", split_axis=0, concat_axis=0, tiled=True)
    spread_other = lax.ppermute(spread, "tile", SWAP)
    held = frame_slot.reshape(FRAME_DEVS, 2, PAIRS, 2).transpose(1, 2, 0, 3)
    held = jnp.where(tile == 0, held, held[::-1]).reshape(1, 768)
    mixed = mix(clip_lengths, held, spread, spread_other, time_taps)
    home = lax.all_to_all(mixed, "frame", split_axis=0, concat_axis=0, tiled=True)
    return project(home, w_proj)


def solution(mesh):
    in_specs = (P("frame", "tile", None), P(), P(), P(), P(), P(), P(None, "tile"), P(), P(), P())
    return jax.shard_map(
        on_device, mesh=mesh, in_specs=in_specs, out_specs=P("frame", None, "tile"), check_vma=False
    )
```

```python
import math

import jax
import jax.numpy as jnp
from jax import lax
from jax.experimental import pallas as pl
from jax.experimental.pallas import tpu as pltpu
from jax.sharding import PartitionSpec as P

D = 1152
HEADS = 16
HEAD_DIM = 72
PATCH = 256
HALF = 128
BLOCKS = 64
FRAMES = 384
FRAME_DEVS = 64
CLIPS = 6
FR_DEV = 6
SLOT_DEV = 12
SLOTS = 768
PAIRS = 3
OUT_DEV = 1792
NORM_EPS = 1e-6
SCORE_SCALE = math.log2(math.e) / math.sqrt(HEAD_DIM)
ENCODE_VMEM = 34 << 20
SMALL_VMEM = 20 << 20

bf16 = jnp.bfloat16
f32 = jnp.float32
NT = (((1,), (1,)), ((), ()))


def resident(shape):
    return pl.BlockSpec(shape, lambda *_: (0,) * len(shape), pipeline_mode=pl.Buffered(1))


def anywhere():
    return pl.BlockSpec(memory_space=pl.ANY)


def head_lanes(head):
    first, last = HEAD_DIM * head, HEAD_DIM * (head + 1) - 1
    return first // 128 * 128, (last // 128 + 1) * 128


def in_vmem(x):
    return pltpu.with_memory_space_constraint(x, pltpu.VMEM)


def normalise(pieces, gain_ref, bias_ref, normed_s):
    gain, bias = gain_ref[...].reshape(1, D), bias_ref[...].reshape(1, D)
    for n, piece in enumerate(pieces):
        rows = piece[...].astype(f32)
        centred = rows - jnp.sum(rows, -1, keepdims=True) * (1.0 / D)
        variance = jnp.sum(centred * centred, -1, keepdims=True) * (1.0 / D)
        normed = centred * lax.rsqrt(variance + NORM_EPS) * gain + bias
        normed_s[n * HALF : (n + 1) * HALF, :] = normed.astype(bf16)


def project_qkv(normed_s, w_ref, qk_s, vt_s):
    for lo in range(0, 3 * D, 256):
        hi = min(lo + 256, 3 * D)
        part = jnp.dot(normed_s[...], w_ref[:, lo:hi], preferred_element_type=f32)
        if hi <= 2 * D:
            qk_s[:, lo:hi] = part.astype(bf16)
        else:
            vt_s[lo - 2 * D : hi - 2 * D, :] = part.T.astype(bf16)


def attend(qk_s, vt_s, ctx_s):
    lane = lax.broadcasted_iota(jnp.int32, (1, D), 1)
    ones = jnp.ones((16, PATCH), bf16)

    def scores(s, head):
        lo, hi = head_lanes(head)
        start = HEAD_DIM * head
        mine = (lane[:, lo:hi] >= start) & (lane[:, lo:hi] < start + HEAD_DIM)
        rows = slice(s * PATCH, (s + 1) * PATCH)
        keys = qk_s[rows, D + lo : D + hi]
        keys = jnp.where(mine, keys, jnp.zeros_like(keys))
        return lax.dot_general(keys, qk_s[rows, lo:hi], NT, preferred_element_type=f32)

    def weigh(score):
        top = jnp.max(score, 0, keepdims=True)
        return jnp.exp2((score - top) * SCORE_SCALE).astype(bf16)

    def total(s, head, weights):
        skip = 8 * (head % 2)
        first = HEAD_DIM * head - skip
        cols = slice(s * PATCH, (s + 1) * PATCH)
        values = jnp.concatenate([vt_s[first : first + 80, cols], ones], 0)
        summed = jnp.dot(values, weights, preferred_element_type=f32)
        ctx_s[HEAD_DIM * head : HEAD_DIM * (head + 1), cols] = (
            summed[skip : skip + HEAD_DIM] / summed[80:81]
        )

    items = [(s, head) for s in range(2) for head in range(HEADS)]
    score, weights = {}, {}
    for n in range(-4, len(items)):
        if n + 4 < len(items):
            score[n + 4] = scores(*items[n + 4])
        if 0 <= n + 2 < len(items):
            weights[n + 2] = weigh(score.pop(n + 2))
        if n >= 0:
            total(*items[n], weights.pop(n))


def pooling(tile, map_ref):
    block = lax.broadcasted_iota(jnp.int32, (BLOCKS, 2 * PATCH), 0)
    col = lax.broadcasted_iota(jnp.int32, (BLOCKS, 2 * PATCH), 1)
    col_block = (col % HALF) // 4 + BLOCKS // 2 * ((col // HALF + tile) % 2)
    row = lax.broadcasted_iota(jnp.int32, (2 * BLOCKS, 1), 0)
    placing = jnp.where(map_ref[...] == row // 2, 1.0, 0.0).astype(bf16)
    member = jnp.where(block == col_block, 0.25, 0.0).astype(bf16)
    member = jnp.dot(placing, member, preferred_element_type=f32)
    frame_of = lax.broadcasted_iota(jnp.int32, (1, 2 * PATCH), 1) // PATCH
    return jnp.where(frame_of == row % 2, member, 0.0).astype(bf16)


def encode_kernel(
    tile_ref, own_ref, other_ref, gain_ref, bias_ref, wqkv_ref, wout_ref, map_ref, out_ref,
    normed_s, qk_s, vt_s, ctx_s, pooled_x, pooled_ctx, pool_s,
):
    pool_s[...] = pooling(tile_ref[0], map_ref)

    def one_pair(pair, carry):
        pieces = [ref.at[2 * pair + s] for s in range(2) for ref in (own_ref, other_ref)]
        normalise(pieces, gain_ref, bias_ref, normed_s)
        project_qkv(normed_s, wqkv_ref, qk_s, vt_s)
        attend(qk_s, vt_s, ctx_s)
        rows = pl.ds(pl.multiple_of(pair * 2 * BLOCKS, 2 * BLOCKS), 2 * BLOCKS)
        pooled = lax.dot_general(
            pool_s[...], ctx_s[...].astype(bf16), NT, preferred_element_type=f32
        )
        pooled_ctx[rows, :] = pooled.astype(bf16)
        patches = jnp.concatenate([piece[...] for piece in pieces], 0)
        pooled_x[rows, :] = jnp.dot(pool_s[...], patches, preferred_element_type=f32)
        return carry

    lax.fori_loop(0, PAIRS, one_pair, 0)
    for pair in range(PAIRS):
        rows = slice(pair * 2 * BLOCKS, (pair + 1) * 2 * BLOCKS)
        total = jnp.dot(pooled_ctx[rows, :], wout_ref[...], preferred_element_type=f32)
        total = (total + pooled_x[rows, :]).astype(bf16)
        out_ref[:, :, pair * D : (pair + 1) * D] = total.reshape(BLOCKS, 2, D)


def encode(tile, own, other, gain, bias, w_qkv, w_out, block_map):
    vmem = pl.BlockSpec(memory_space=pltpu.VMEM)
    return pl.pallas_call(
        encode_kernel,
        in_specs=[pl.BlockSpec(memory_space=pltpu.SMEM)] + [vmem] * 7,
        out_specs=vmem,
        out_shape=jax.ShapeDtypeStruct((BLOCKS, 2, PAIRS * D), bf16),
        scratch_shapes=[
            pltpu.VMEM((2 * PATCH, D), bf16),
            pltpu.VMEM((2 * PATCH, 2 * D), bf16),
            pltpu.VMEM((D, 2 * PATCH), bf16),
            pltpu.VMEM((D, 2 * PATCH), f32),
            pltpu.VMEM((PAIRS * 2 * BLOCKS, D), f32),
            pltpu.VMEM((PAIRS * 2 * BLOCKS, D), bf16),
            pltpu.VMEM((2 * BLOCKS, 2 * PATCH), bf16),
        ],
        compiler_params=pltpu.CompilerParams(vmem_limit_bytes=ENCODE_VMEM),
        name="encode_frames",
    )(tile, in_vmem(own), in_vmem(other), gain, bias, in_vmem(w_qkv), in_vmem(w_out), block_map)


def mix_kernel(tile_ref, lengths_ref, slots_ref, own_ref, other_ref, taps_ref, out_ref, rows_s, held_s):
    step = pl.program_id(0)

    @pl.when(step == 0)
    def _():
        for j in range(PAIRS):
            cols = slice(j * D, (j + 1) * D)
            rows_s[j * 128 : (j + 1) * 128, :] = own_ref[:, :, cols].reshape(128, D)
            rows_s[(j + 3) * 128 : (j + 4) * 128, :] = other_ref[:, :, cols].reshape(128, D)
        code = slots_ref[...] + 1
        code = jnp.concatenate([code // 16, code % 16] + [jnp.zeros_like(code)] * 6, 0)
        slot = lax.broadcasted_iota(jnp.int32, (SLOTS, SLOTS), 0)
        col = lax.broadcasted_iota(jnp.int32, (1, SLOTS), 1)
        group, place = col // 128, col % 128
        core = (group // PAIRS + tile_ref[0]) % 2
        source = SLOT_DEV * (place // 2) + FR_DEV * core + 2 * (group % PAIRS) + place % 2
        moved = jnp.where(slot == source, 1.0, 0.0).astype(bf16)
        code = jnp.dot(code.astype(f32).astype(bf16), moved, preferred_element_type=f32)
        held_s[...] = (code[0:1] * 16.0 + code[1:2]).astype(jnp.int32) - 1

    row = lax.broadcasted_iota(jnp.int32, (128, 1), 0)
    frame = FR_DEV * (row // 2) + 2 * step + row % 2
    first, last = frame < 0, frame + 1 == FRAMES
    start = 0
    for c in range(CLIPS):
        first |= frame == start
        last |= frame + 1 == start
        start += lengths_ref[c]
    held = held_s[...]

    def pick(wanted):
        hit = jnp.where(held == wanted, 1.0, 0.0).astype(bf16)
        return jnp.dot(hit, rows_s[...], preferred_element_type=f32)

    earlier = pick(jnp.where(first, -2, frame - 1))
    later = pick(jnp.where(last, -2, frame + 1))
    mixed = taps_ref[0:1] * earlier + taps_ref[1:2] * pick(frame) + taps_ref[2:3] * later
    out_ref[...] = mixed.astype(bf16).reshape(FRAME_DEVS, 2, D)


def mix(tile, lengths, slots, own, other, taps):
    return pl.pallas_call(
        mix_kernel,
        grid=(PAIRS,),
        in_specs=[
            pl.BlockSpec(memory_space=pltpu.SMEM),
            pl.BlockSpec(memory_space=pltpu.SMEM),
            resident((1, SLOTS)),
            resident((FRAME_DEVS, 2, PAIRS * D)),
            resident((FRAME_DEVS, 2, PAIRS * D)),
            resident((3, D)),
        ],
        out_specs=pl.BlockSpec((FRAME_DEVS, 2, D), lambda i: (0, 0, i)),
        out_shape=jax.ShapeDtypeStruct((FRAME_DEVS, 2, PAIRS * D), bf16),
        scratch_shapes=[pltpu.VMEM((SLOTS, D), bf16), pltpu.VMEM((1, SLOTS), jnp.int32)],
        compiler_params=pltpu.CompilerParams(vmem_limit_bytes=SMALL_VMEM),
        name="mix_rows",
    )(tile, lengths, slots, own, other, taps)


def project_kernel(mixed_ref, w_ref, out_ref):
    row = lax.broadcasted_iota(jnp.int32, (128, 128), 0)
    col = lax.broadcasted_iota(jnp.int32, (128, 128), 1)
    swap = jnp.where(col == 2 * (row % BLOCKS) + row // BLOCKS, 1.0, 0.0).astype(bf16)
    rows = mixed_ref[...].reshape(128, D)
    rows = jnp.dot(swap, rows, preferred_element_type=f32).astype(bf16)
    out = jnp.dot(rows, w_ref[...], preferred_element_type=f32).astype(bf16)
    out_ref[...] = out.reshape(2, BLOCKS, OUT_DEV)


def project(mixed, w_proj):
    return pl.pallas_call(
        project_kernel,
        grid=(PAIRS,),
        in_specs=[
            pl.BlockSpec((BLOCKS, 2, D), lambda i: (0, 0, i)),
            resident((D, OUT_DEV)),
        ],
        out_specs=pl.BlockSpec((2, BLOCKS, OUT_DEV), lambda i: (i, 0, 0)),
        out_shape=jax.ShapeDtypeStruct((FR_DEV, BLOCKS, OUT_DEV), bf16),
        compiler_params=pltpu.CompilerParams(vmem_limit_bytes=SMALL_VMEM),
        name="project_rows",
    )(mixed, w_proj)


SWAP = [(0, 1), (1, 0)]


def on_device(
    frames_in, norm_gain, norm_bias, w_qkv, w_out, time_taps, w_proj, clip_lengths, frame_slot, block_map
):
    tile = lax.axis_index("tile")
    sent = lax.dynamic_slice_in_dim(frames_in, FR_DEV * (1 - tile), FR_DEV)
    other = lax.ppermute(sent, "tile", SWAP)
    core = jnp.reshape(tile, (1,)).astype(jnp.int32)
    own = lax.dynamic_slice_in_dim(frames_in, FR_DEV * tile, FR_DEV)
    pooled = encode(
        core, own, other, norm_gain, norm_bias, w_qkv, w_out, block_map[None]
    )
    spread = lax.all_to_all(pooled, "frame", split_axis=0, concat_axis=0, tiled=True)
    spread_other = lax.ppermute(spread, "tile", SWAP)
    mixed = mix(core, clip_lengths, frame_slot[None], spread, spread_other, time_taps)
    home = lax.all_to_all(mixed, "frame", split_axis=0, concat_axis=0, tiled=True)
    return project(home, w_proj)


def solution(mesh):
    in_specs = (P("frame", "tile", None), P(), P(), P(), P(), P(), P(None, "tile"), P(), P(), P())
    return jax.shard_map(
        on_device, mesh=mesh, in_specs=in_specs, out_specs=P("frame", None, "tile"), check_vma=False
    )
```

```python
import math

import jax
import jax.numpy as jnp
from jax import lax
from jax.experimental import pallas as pl
from jax.experimental.pallas import tpu as pltpu
from jax.sharding import PartitionSpec as P

D = 1152
HEADS = 16
HEAD_DIM = 72
PATCH = 256
HALF = 128
BLOCKS = 64
FRAMES = 384
FRAME_DEVS = 64
CLIPS = 6
FR_DEV = 6
SLOT_DEV = 12
SLOTS = 768
PAIRS = 3
PART = 640
REST = 512
OUT_CUT = 896
OUT_DEV = 1792
NORM_EPS = 1e-6
SCORE_SCALE = math.log2(math.e) / math.sqrt(HEAD_DIM)
STAGE_VMEM = 16 << 20
ENCODE_VMEM = 34 << 20
SMALL_VMEM = 16 << 20

bf16 = jnp.bfloat16
f32 = jnp.float32
NT = (((1,), (1,)), ((), ()))


def head_lanes(head):
    first, last = HEAD_DIM * head, HEAD_DIM * (head + 1) - 1
    return first // 128 * 128, (last // 128 + 1) * 128


def in_vmem(x):
    return pltpu.with_memory_space_constraint(x, pltpu.VMEM)


def in_hbm(x):
    return pltpu.with_memory_space_constraint(x, pltpu.HBM)


def normalise(rows, gain_ref, bias_ref):
    gain, bias = gain_ref[...].reshape(1, D), bias_ref[...].reshape(1, D)
    rows = rows.astype(f32)
    centred = rows - jnp.sum(rows, -1, keepdims=True) * (1.0 / D)
    variance = jnp.sum(centred * centred, -1, keepdims=True) * (1.0 / D)
    return (centred * lax.rsqrt(variance + NORM_EPS) * gain + bias).astype(bf16)


def stage_kernel(
    tile_ref, frames_any, gain_ref, bias_ref, wqkv_any, wout_any,
    own_ref, normed_ref, wqkv_ref, wout_ref, sems,
):
    rows = pl.ds(FR_DEV * tile_ref[0], FR_DEV)
    copies = [pltpu.make_async_copy(frames_any.at[rows], own_ref, sems.at[0])]
    step = D // 4
    for n in range(4):
        part = pl.ds(n * step, step)
        copies.append(pltpu.make_async_copy(wqkv_any.at[part], wqkv_ref.at[part], sems.at[n + 1]))
    copies.append(pltpu.make_async_copy(wout_any, wout_ref, sems.at[5]))
    for copy in copies:
        copy.start()
    copies[0].wait()
    for f in range(FR_DEV):
        normed_ref[f] = normalise(own_ref[f], gain_ref, bias_ref)
    for copy in copies[1:]:
        copy.wait()


def stage(tile, frames_in, gain, bias, w_qkv, w_out):
    smem, vmem, hbm = (pl.BlockSpec(memory_space=m) for m in (pltpu.SMEM, pltpu.VMEM, pltpu.HBM))
    return pl.pallas_call(
        stage_kernel,
        in_specs=[smem, hbm, vmem, vmem, hbm, hbm],
        out_specs=[vmem] * 4,
        out_shape=[
            pltpu.VMEM((FR_DEV, HALF, D), bf16),
            pltpu.VMEM((FR_DEV, HALF, D), bf16),
            pltpu.VMEM((D, 3 * D), bf16),
            pltpu.VMEM((D, D), bf16),
        ],
        scratch_shapes=[pltpu.SemaphoreType.DMA((6,))],
        compiler_params=pltpu.CompilerParams(vmem_limit_bytes=STAGE_VMEM),
        name="stage_operands",
    )(tile, in_hbm(frames_in), gain, bias, in_hbm(w_qkv), in_hbm(w_out))


def project_qkv(normed_s, w_ref, qk_s, vt_s):
    for lo in range(0, 3 * D, 256):
        hi = min(lo + 256, 3 * D)
        part = jnp.dot(normed_s[...], w_ref[:, lo:hi], preferred_element_type=f32)
        if hi <= 2 * D:
            qk_s[:, lo:hi] = part.astype(bf16)
        else:
            vt_s[lo - 2 * D : hi - 2 * D, :] = part.T.astype(bf16)


def attend(qk_s, vt_s, ctx_s):
    lane = lax.broadcasted_iota(jnp.int32, (1, D), 1)
    ones = jnp.ones((16, PATCH), bf16)

    def scores(s, head):
        lo, hi = head_lanes(head)
        start = HEAD_DIM * head
        mine = (lane[:, lo:hi] >= start) & (lane[:, lo:hi] < start + HEAD_DIM)
        rows = slice(s * PATCH, (s + 1) * PATCH)
        keys = qk_s[rows, D + lo : D + hi]
        keys = jnp.where(mine, keys, jnp.zeros_like(keys))
        return lax.dot_general(keys, qk_s[rows, lo:hi], NT, preferred_element_type=f32)

    def weigh(score):
        top = jnp.max(score, 0, keepdims=True)
        return jnp.exp2((score - top) * SCORE_SCALE).astype(bf16)

    def total(s, head, weights):
        skip = 8 * (head % 2)
        first = HEAD_DIM * head - skip
        cols = slice(s * PATCH, (s + 1) * PATCH)
        values = jnp.concatenate([vt_s[first : first + 80, cols], ones], 0)
        summed = jnp.dot(values, weights, preferred_element_type=f32)
        ctx_s[HEAD_DIM * head : HEAD_DIM * (head + 1), cols] = (
            summed[skip : skip + HEAD_DIM] / summed[80:81]
        )

    items = [(s, head) for s in range(2) for head in range(HEADS)]
    score, weights = {}, {}
    for n in range(-4, len(items)):
        if n + 4 < len(items):
            score[n + 4] = scores(*items[n + 4])
        if 0 <= n + 2 < len(items):
            weights[n + 2] = weigh(score.pop(n + 2))
        if n >= 0:
            total(*items[n], weights.pop(n))


def pooling(tile, map_ref):
    block = lax.broadcasted_iota(jnp.int32, (BLOCKS, 2 * PATCH), 0)
    col = lax.broadcasted_iota(jnp.int32, (BLOCKS, 2 * PATCH), 1)
    col_block = (col % HALF) // 4 + BLOCKS // 2 * ((col // HALF + tile) % 2)
    row = lax.broadcasted_iota(jnp.int32, (2 * BLOCKS, 1), 0)
    placing = jnp.where(map_ref[...] == row // 2, 1.0, 0.0).astype(bf16)
    member = jnp.where(block == col_block, 0.25, 0.0).astype(bf16)
    member = jnp.dot(placing, member, preferred_element_type=f32)
    frame_of = lax.broadcasted_iota(jnp.int32, (1, 2 * PATCH), 1) // PATCH
    return jnp.where(frame_of == row % 2, member, 0.0).astype(bf16)


def encode_kernel(
    tile_ref, own_ref, own_normed, other_ref, gain_ref, bias_ref, wqkv_ref, wout_ref, map_ref, out_ref,
    normed_s, qk_s, vt_s, ctx_s, pooled_x, pooled_ctx, pool_s,
):
    pool_s[...] = pooling(tile_ref[0], map_ref)

    def one_pair(pair, carry):
        for s in range(2):
            frame = 2 * pair + s
            mid = s * PATCH + HALF
            normed_s[s * PATCH : mid, :] = own_normed[frame]
            normed_s[mid : (s + 1) * PATCH, :] = normalise(other_ref[frame], gain_ref, bias_ref)
        project_qkv(normed_s, wqkv_ref, qk_s, vt_s)
        attend(qk_s, vt_s, ctx_s)
        rows = pl.ds(pl.multiple_of(pair * 2 * BLOCKS, 2 * BLOCKS), 2 * BLOCKS)
        pooled = lax.dot_general(
            pool_s[...], ctx_s[...].astype(bf16), NT, preferred_element_type=f32
        )
        pooled_ctx[rows, :] = pooled.astype(bf16)
        patches = [ref[2 * pair + s] for s in range(2) for ref in (own_ref, other_ref)]
        patches = jnp.concatenate(patches, 0)
        pooled_x[rows, :] = jnp.dot(pool_s[...], patches, preferred_element_type=f32)
        return carry

    lax.fori_loop(0, PAIRS, one_pair, 0)
    for pair in range(PAIRS):
        rows = slice(pair * 2 * BLOCKS, (pair + 1) * 2 * BLOCKS)
        total = jnp.dot(pooled_ctx[rows, :], wout_ref[...], preferred_element_type=f32)
        total = (total + pooled_x[rows, :]).astype(bf16)
        out_ref[:, :, pair * D : (pair + 1) * D] = total.reshape(BLOCKS, 2, D)


def encode(tile, own, own_normed, other, gain, bias, w_qkv, w_out, block_map):
    vmem = pl.BlockSpec(memory_space=pltpu.VMEM)
    return pl.pallas_call(
        encode_kernel,
        in_specs=[pl.BlockSpec(memory_space=pltpu.SMEM)] + [vmem] * 8,
        out_specs=vmem,
        out_shape=pltpu.VMEM((BLOCKS, 2, PAIRS * D), bf16),
        scratch_shapes=[
            pltpu.VMEM((2 * PATCH, D), bf16),
            pltpu.VMEM((2 * PATCH, 2 * D), bf16),
            pltpu.VMEM((D, 2 * PATCH), bf16),
            pltpu.VMEM((D, 2 * PATCH), f32),
            pltpu.VMEM((PAIRS * 2 * BLOCKS, D), f32),
            pltpu.VMEM((PAIRS * 2 * BLOCKS, D), bf16),
            pltpu.VMEM((2 * BLOCKS, 2 * PATCH), bf16),
        ],
        compiler_params=pltpu.CompilerParams(vmem_limit_bytes=ENCODE_VMEM),
        name="encode_frames",
    )(
        tile, in_vmem(own), in_vmem(own_normed), in_vmem(other), gain, bias,
        in_vmem(w_qkv), in_vmem(w_out), block_map,
    )


def own_rows(ref, rows_s, tile):
    for j in range(PAIRS):
        cols = pl.ds(pl.multiple_of(j * D + 512 * tile, 128), PART)
        rows_s[j * 128 : (j + 1) * 128, :] = ref[:, :, cols].reshape(128, PART)


def pick_kernel(
    tile_ref, lengths_ref, slots_ref, own_ref, other_hit, picked_ref, rows_s, own_hit
):
    tile = tile_ref[0]
    own_rows(own_ref, rows_s, tile)
    code = slots_ref[...] + 1
    code = jnp.concatenate([code // 16, code % 16] + [jnp.zeros_like(code)] * 6, 0)
    slot = lax.broadcasted_iota(jnp.int32, (SLOTS, SLOTS), 0)
    col = lax.broadcasted_iota(jnp.int32, (1, SLOTS), 1)
    group, place = col // 128, col % 128
    core = (group // PAIRS + tile) % 2
    source = SLOT_DEV * (place // 2) + FR_DEV * core + 2 * (group % PAIRS) + place % 2
    moved = jnp.where(slot == source, 1.0, 0.0).astype(bf16)
    code = jnp.dot(code.astype(f32).astype(bf16), moved, preferred_element_type=f32)
    held = (code[0:1] * 16.0 + code[1:2]).astype(jnp.int32) - 1
    row = lax.broadcasted_iota(jnp.int32, (128, 1), 0)
    for step in range(PAIRS):
        frame = FR_DEV * (row // 2) + 2 * step + row % 2
        first, last = frame < 0, frame + 1 == FRAMES
        start = 0
        for c in range(CLIPS):
            first |= frame == start
            last |= frame + 1 == start
            start += lengths_ref[c]
        wanted = (jnp.where(first, -2, frame - 1), frame, jnp.where(last, -2, frame + 1))
        for tap, want in enumerate(wanted):
            rows = slice((PAIRS * step + tap) * 128, (PAIRS * step + tap + 1) * 128)
            hit = jnp.where(held == want, 1.0, 0.0).astype(bf16)
            own_hit[rows, :] = hit[:, : SLOTS // 2]
            other_hit[rows, :] = hit[:, SLOTS // 2 :]
    picked_ref[...] = jnp.dot(own_hit[...], rows_s[...], preferred_element_type=f32)


def pick(tile, lengths, slots, own):
    smem, vmem = (pl.BlockSpec(memory_space=m) for m in (pltpu.SMEM, pltpu.VMEM))
    return pl.pallas_call(
        pick_kernel,
        in_specs=[smem, smem, vmem, vmem],
        out_specs=[vmem, vmem],
        out_shape=[
            pltpu.VMEM((9 * 128, SLOTS // 2), bf16),
            pltpu.VMEM((9 * 128, PART), f32),
        ],
        scratch_shapes=[
            pltpu.VMEM((SLOTS // 2, PART), bf16),
            pltpu.VMEM((9 * 128, SLOTS // 2), bf16),
        ],
        compiler_params=pltpu.CompilerParams(vmem_limit_bytes=SMALL_VMEM),
        name="pick_own_rows",
    )(tile, lengths, slots, in_vmem(own))


def mix_kernel(tile_ref, other_ref, other_hit, picked_ref, taps_ref, out_ref, rows_s, picked_s):
    tile = tile_ref[0]
    own_rows(other_ref, rows_s, tile)
    picked_s[...] = jnp.dot(other_hit[...], rows_s[...], preferred_element_type=f32)
    taps = taps_ref[:, pl.ds(pl.multiple_of(512 * tile, 128), PART)]
    for step in range(PAIRS):
        mixed = 0.0
        for tap in range(3):
            first = (PAIRS * step + tap) * 128
            rows = slice(first, first + 128)
            mixed += taps[tap : tap + 1] * (picked_s[rows, :] + picked_ref[rows, :])
        mixed = mixed.astype(bf16).reshape(FRAME_DEVS, 2, PART)
        out_ref[:, :, step * PART : (step + 1) * PART] = mixed


def mix(tile, other, other_hit, picked, taps):
    smem, vmem = (pl.BlockSpec(memory_space=m) for m in (pltpu.SMEM, pltpu.VMEM))
    return pl.pallas_call(
        mix_kernel,
        in_specs=[smem, vmem, vmem, vmem, vmem],
        out_specs=vmem,
        out_shape=pltpu.VMEM((FRAME_DEVS, 2, PAIRS * PART), bf16),
        scratch_shapes=[
            pltpu.VMEM((SLOTS // 2, PART), bf16),
            pltpu.VMEM((9 * 128, PART), f32),
        ],
        compiler_params=pltpu.CompilerParams(vmem_limit_bytes=SMALL_VMEM),
        name="mix_rows",
    )(tile, in_vmem(other), in_vmem(other_hit), in_vmem(picked), taps)


def deinterleave(rows):
    row = lax.broadcasted_iota(jnp.int32, (128, 128), 0)
    col = lax.broadcasted_iota(jnp.int32, (128, 128), 1)
    order = jnp.where(col == 2 * (row % BLOCKS) + row // BLOCKS, 1.0, 0.0).astype(bf16)
    return jnp.dot(order, rows, preferred_element_type=f32).astype(bf16)


def project_own_kernel(tile_ref, own_ref, w_ref, part_ref, rows_s):
    for j in range(PAIRS):
        rows = own_ref[:, :, j * PART : (j + 1) * PART].reshape(128, PART)
        rows_s[j * 128 : (j + 1) * 128, :] = deinterleave(rows)
    first = pl.multiple_of(512 * tile_ref[0], 128)
    for lo in range(0, OUT_DEV, 256):
        weights = w_ref[pl.ds(first, PART), lo : lo + 256]
        part_ref[:, lo : lo + 256] = jnp.dot(rows_s[...], weights, preferred_element_type=f32)


def project_own(tile, own, w_proj):
    smem, vmem = (pl.BlockSpec(memory_space=m) for m in (pltpu.SMEM, pltpu.VMEM))
    return pl.pallas_call(
        project_own_kernel,
        in_specs=[smem, vmem, vmem],
        out_specs=vmem,
        out_shape=pltpu.VMEM((FR_DEV * BLOCKS, OUT_DEV), f32),
        scratch_shapes=[pltpu.VMEM((FR_DEV * BLOCKS, PART), bf16)],
        compiler_params=pltpu.CompilerParams(vmem_limit_bytes=SMALL_VMEM),
        name="project_own_channels",
    )(tile, in_vmem(own), in_vmem(w_proj))


def project_kernel(tile_ref, other_ref, part_ref, w_ref, out_hbm, rows_s, out_s, sems):
    tile = tile_ref[0]
    for j in range(PAIRS):
        cols = pl.ds(pl.multiple_of(j * PART + 128 * (1 - tile), 128), REST)
        rows_s[j * 128 : (j + 1) * 128, :] = deinterleave(other_ref[:, :, cols].reshape(128, REST))
    first = pl.multiple_of(PART * (1 - tile), 128)
    copies = []
    for n, lo in enumerate(range(0, OUT_DEV, OUT_CUT)):
        for mid in range(lo, lo + OUT_CUT, 256):
            cols = slice(mid, min(mid + 256, lo + OUT_CUT))
            weights = w_ref[pl.ds(first, REST), cols]
            out = jnp.dot(rows_s[...], weights, preferred_element_type=f32) + part_ref[:, cols]
            out_s[:, :, cols] = out.astype(bf16).reshape(FR_DEV, BLOCKS, cols.stop - cols.start)
        cols = pl.ds(lo, OUT_CUT)
        copies.append(
            pltpu.make_async_copy(out_s.at[:, :, cols], out_hbm.at[:, :, cols], sems.at[n])
        )
        copies[n].start()
    for copy in copies:
        copy.wait()


def project(tile, other, part, w_proj):
    smem, vmem = (pl.BlockSpec(memory_space=m) for m in (pltpu.SMEM, pltpu.VMEM))
    shape = (FR_DEV, BLOCKS, OUT_DEV)
    return pl.pallas_call(
        project_kernel,
        in_specs=[smem, vmem, vmem, vmem],
        out_specs=pl.BlockSpec(memory_space=pltpu.HBM),
        out_shape=jax.ShapeDtypeStruct(shape, bf16),
        scratch_shapes=[
            pltpu.VMEM((FR_DEV * BLOCKS, REST), bf16),
            pltpu.VMEM(shape, bf16),
            pltpu.SemaphoreType.DMA((OUT_DEV // OUT_CUT,)),
        ],
        compiler_params=pltpu.CompilerParams(vmem_limit_bytes=SMALL_VMEM),
        name="project_rows",
    )(tile, in_vmem(other), in_vmem(part), in_vmem(w_proj))


SWAP = [(0, 1), (1, 0)]


def on_device(
    frames_in, norm_gain, norm_bias, w_qkv, w_out, time_taps, w_proj, clip_lengths, frame_slot, block_map
):
    tile = lax.axis_index("tile")
    sent = lax.dynamic_slice_in_dim(frames_in, FR_DEV * (1 - tile), FR_DEV)
    other = lax.ppermute(sent, "tile", SWAP)
    core = jnp.reshape(tile, (1,)).astype(jnp.int32)
    core = jnp.reshape(tile, (1,)).astype(jnp.int32)
    frames_in, _ = lax.optimization_barrier((frames_in, sent))
    own, own_normed, w_qkv, w_out = stage(core, frames_in, norm_gain, norm_bias, w_qkv, w_out)
    pooled = encode(
        core, own, own_normed, other, norm_gain, norm_bias, w_qkv, w_out, block_map[None]
    )
    spread = lax.all_to_all(pooled, "frame", split_axis=0, concat_axis=0, tiled=True)
    spread_other = lax.ppermute(spread, "tile", SWAP)
    other_hit, picked = pick(core, clip_lengths, frame_slot[None], spread)
    mixed = mix(core, spread_other, other_hit, picked, time_taps)
    home = lax.all_to_all(mixed, "frame", split_axis=0, concat_axis=0, tiled=True)
    home_other = lax.ppermute(home, "tile", SWAP)
    part = project_own(core, home, w_proj)
    return project(core, home_other, part, w_proj)


def solution(mesh):
    in_specs = (P("frame", "tile", None), P(), P(), P(), P(), P(), P(None, "tile"), P(), P(), P())
    return jax.shard_map(
        on_device, mesh=mesh, in_specs=in_specs, out_specs=P("frame", None, "tile"), check_vma=False
    )
```

```python
import math

import jax
import jax.numpy as jnp
from jax import lax
from jax.experimental import pallas as pl
from jax.experimental.pallas import tpu as pltpu
from jax.sharding import PartitionSpec as P

D = 1152
HEADS = 16
HEAD_DIM = 72
PATCH = 256
HALF = 128
BLOCKS = 64
FRAMES = 384
FRAME_DEVS = 64
CLIPS = 6
FR_DEV = 6
SLOT_DEV = 12
SLOTS = 768
PAIRS = 3
PART = 640
REST = 512
OUT_CUT = 896
OUT_DEV = 1792
NORM_EPS = 1e-6
SCORE_SCALE = math.log2(math.e) / math.sqrt(HEAD_DIM)
STAGE_VMEM = 16 << 20
ENCODE_VMEM = 34 << 20
SMALL_VMEM = 16 << 20

bf16 = jnp.bfloat16
f32 = jnp.float32
NT = (((1,), (1,)), ((), ()))


def head_lanes(head):
    first, last = HEAD_DIM * head, HEAD_DIM * (head + 1) - 1
    return first // 128 * 128, (last // 128 + 1) * 128


def in_vmem(x):
    return pltpu.with_memory_space_constraint(x, pltpu.VMEM)


def in_hbm(x):
    return pltpu.with_memory_space_constraint(x, pltpu.HBM)


def normalise(rows, gain_ref, bias_ref):
    gain, bias = gain_ref[...].reshape(1, D), bias_ref[...].reshape(1, D)
    rows = rows.astype(f32)
    centred = rows - jnp.sum(rows, -1, keepdims=True) * (1.0 / D)
    variance = jnp.sum(centred * centred, -1, keepdims=True) * (1.0 / D)
    return (centred * lax.rsqrt(variance + NORM_EPS) * gain + bias).astype(bf16)


def cut_kernel(tile_ref, frames_hbm, out_ref, sems):
    first = FR_DEV * (1 - tile_ref[0])
    copies = []
    for f in range(FR_DEV):
        copies.append(
            pltpu.make_async_copy(frames_hbm.at[first + f], out_ref.at[f], sems.at[f])
        )
        copies[f].start()
    for copy in copies:
        copy.wait()


def cut_sent(tile, frames_in):
    return pl.pallas_call(
        cut_kernel,
        in_specs=[pl.BlockSpec(memory_space=m) for m in (pltpu.SMEM, pltpu.HBM)],
        out_specs=pl.BlockSpec(memory_space=pltpu.VMEM),
        out_shape=pltpu.VMEM((FR_DEV, HALF, D), bf16),
        scratch_shapes=[pltpu.SemaphoreType.DMA((FR_DEV,))],
        compiler_params=pltpu.CompilerParams(vmem_limit_bytes=STAGE_VMEM),
        name="cut_sent_half",
    )(tile, in_hbm(frames_in))


def stage_kernel(
    tile_ref, frames_hbm, gain_ref, bias_ref, map_ref, wqkv_hbm,
    own_ref, normed_ref, wqkv_ref, pool_ref, sems,
):
    rows = pl.ds(FR_DEV * tile_ref[0], FR_DEV)
    copies = [pltpu.make_async_copy(frames_hbm.at[rows], own_ref, sems.at[0])]
    step = D // 4
    for n in range(4):
        part = pl.ds(n * step, step)
        copies.append(pltpu.make_async_copy(wqkv_hbm.at[part], wqkv_ref.at[part], sems.at[n + 1]))
    for copy in copies:
        copy.start()
    pool_ref[...] = pooling(tile_ref[0], map_ref)
    copies[0].wait()
    for f in range(FR_DEV):
        normed_ref[f] = normalise(own_ref[f], gain_ref, bias_ref)
    for copy in copies[1:]:
        copy.wait()


def stage(tile, frames_in, gain, bias, block_map, w_qkv):
    smem, vmem, hbm = (pl.BlockSpec(memory_space=m) for m in (pltpu.SMEM, pltpu.VMEM, pltpu.HBM))
    return pl.pallas_call(
        stage_kernel,
        in_specs=[smem, hbm, vmem, vmem, vmem, hbm],
        out_specs=[vmem] * 4,
        out_shape=[
            pltpu.VMEM((FR_DEV, HALF, D), bf16),
            pltpu.VMEM((FR_DEV, HALF, D), bf16),
            pltpu.VMEM((D, 3 * D), bf16),
            pltpu.VMEM((2 * BLOCKS, 2 * PATCH), bf16),
        ],
        scratch_shapes=[pltpu.SemaphoreType.DMA((5,))],
        compiler_params=pltpu.CompilerParams(vmem_limit_bytes=STAGE_VMEM),
        name="stage_operands",
    )(tile, in_hbm(frames_in), gain, bias, block_map, in_hbm(w_qkv))


def project_qkv(normed_s, w_ref, qk_s, vt_s):
    for lo in range(0, 3 * D, 256):
        hi = min(lo + 256, 3 * D)
        part = jnp.dot(normed_s[...], w_ref[:, lo:hi], preferred_element_type=f32)
        if hi <= 2 * D:
            qk_s[:, lo:hi] = part.astype(bf16)
        else:
            vt_s[lo - 2 * D : hi - 2 * D, :] = part.astype(bf16).T


def attend(qk_s, vt_s, ctx_s):
    lane = lax.broadcasted_iota(jnp.int32, (1, D), 1)
    ones = jnp.ones((16, PATCH), bf16)

    def scores(s, head):
        lo, hi = head_lanes(head)
        start = HEAD_DIM * head
        mine = (lane[:, lo:hi] >= start) & (lane[:, lo:hi] < start + HEAD_DIM)
        rows = slice(s * PATCH, (s + 1) * PATCH)
        keys = qk_s[rows, D + lo : D + hi]
        keys = jnp.where(mine, keys, jnp.zeros_like(keys))
        return lax.dot_general(keys, qk_s[rows, lo:hi], NT, preferred_element_type=f32)

    def weigh(score):
        top = jnp.max(score, 0, keepdims=True)
        return jnp.exp2((score - top) * SCORE_SCALE).astype(bf16)

    def total(s, head, weights):
        skip = 8 * (head % 2)
        first = HEAD_DIM * head - skip
        cols = slice(s * PATCH, (s + 1) * PATCH)
        values = jnp.concatenate([vt_s[first : first + 80, cols], ones], 0)
        summed = jnp.dot(values, weights, preferred_element_type=f32)
        ctx_s[HEAD_DIM * head : HEAD_DIM * (head + 1), cols] = (
            summed[skip : skip + HEAD_DIM] / summed[80:81]
        )

    items = [(s, head) for s in range(2) for head in range(HEADS)]
    score, weights = {}, {}
    for n in range(-6, len(items)):
        if n + 6 < len(items):
            score[n + 6] = scores(*items[n + 6])
        if 0 <= n + 3 < len(items):
            weights[n + 3] = weigh(score.pop(n + 3))
        if n >= 0:
            total(*items[n], weights.pop(n))


def pooling(tile, map_ref):
    block = lax.broadcasted_iota(jnp.int32, (BLOCKS, 2 * PATCH), 0)
    col = lax.broadcasted_iota(jnp.int32, (BLOCKS, 2 * PATCH), 1)
    col_block = (col % HALF) // 4 + BLOCKS // 2 * ((col // HALF + tile) % 2)
    row = lax.broadcasted_iota(jnp.int32, (2 * BLOCKS, 1), 0)
    placing = jnp.where(map_ref[...] == row // 2, 1.0, 0.0).astype(bf16)
    member = jnp.where(block == col_block, 0.25, 0.0).astype(bf16)
    member = jnp.dot(placing, member, preferred_element_type=f32)
    frame_of = lax.broadcasted_iota(jnp.int32, (1, 2 * PATCH), 1) // PATCH
    return jnp.where(frame_of == row % 2, member, 0.0).astype(bf16)


def encode_kernel(
    own_ref, own_normed, other_ref, gain_ref, bias_ref, wqkv_ref, wout_hbm, pool_ref, out_ref,
    wout_s, normed_s, qk_s, vt_s, ctx_s, pooled_x, pooled_ctx, sem,
):
    wout_copy = pltpu.make_async_copy(wout_hbm, wout_s, sem)
    wout_copy.start()

    def one_pair(pair, carry):
        for s in range(2):
            frame = 2 * pair + s
            mid = s * PATCH + HALF
            normed_s[s * PATCH : mid, :] = own_normed[frame]
            normed_s[mid : (s + 1) * PATCH, :] = normalise(other_ref[frame], gain_ref, bias_ref)
        project_qkv(normed_s, wqkv_ref, qk_s, vt_s)
        attend(qk_s, vt_s, ctx_s)
        rows = pl.ds(pl.multiple_of(pair * 2 * BLOCKS, 2 * BLOCKS), 2 * BLOCKS)
        pooled = lax.dot_general(
            pool_ref[...], ctx_s[...].astype(bf16), NT, preferred_element_type=f32
        )
        pooled_ctx[rows, :] = pooled.astype(bf16)
        patches = [ref[2 * pair + s] for s in range(2) for ref in (own_ref, other_ref)]
        patches = jnp.concatenate(patches, 0)
        pooled_x[rows, :] = jnp.dot(pool_ref[...], patches, preferred_element_type=f32)
        return carry

    lax.fori_loop(0, PAIRS, one_pair, 0)
    wout_copy.wait()
    for pair in range(PAIRS):
        rows = slice(pair * 2 * BLOCKS, (pair + 1) * 2 * BLOCKS)
        total = jnp.dot(pooled_ctx[rows, :], wout_s[...], preferred_element_type=f32)
        total = (total + pooled_x[rows, :]).astype(bf16)
        out_ref[:, :, pair * D : (pair + 1) * D] = total.reshape(BLOCKS, 2, D)


def encode(own, own_normed, other, gain, bias, w_qkv, w_out, pool):
    vmem, hbm = (pl.BlockSpec(memory_space=m) for m in (pltpu.VMEM, pltpu.HBM))
    return pl.pallas_call(
        encode_kernel,
        in_specs=[vmem] * 6 + [hbm, vmem],
        out_specs=vmem,
        out_shape=pltpu.VMEM((BLOCKS, 2, PAIRS * D), bf16),
        scratch_shapes=[
            pltpu.VMEM((D, D), bf16),
            pltpu.VMEM((2 * PATCH, D), bf16),
            pltpu.VMEM((2 * PATCH, 2 * D), bf16),
            pltpu.VMEM((D, 2 * PATCH), bf16),
            pltpu.VMEM((D, 2 * PATCH), f32),
            pltpu.VMEM((PAIRS * 2 * BLOCKS, D), f32),
            pltpu.VMEM((PAIRS * 2 * BLOCKS, D), bf16),
            pltpu.SemaphoreType.DMA,
        ],
        compiler_params=pltpu.CompilerParams(vmem_limit_bytes=ENCODE_VMEM),
        name="encode_frames",
    )(
        in_vmem(own), in_vmem(own_normed), in_vmem(other), gain, bias,
        in_vmem(w_qkv), in_hbm(w_out), in_vmem(pool),
    )


def own_rows(ref, rows_s, tile):
    for j in range(PAIRS):
        cols = pl.ds(pl.multiple_of(j * D + 512 * tile, 128), PART)
        rows_s[j * 128 : (j + 1) * 128, :] = ref[:, :, cols].reshape(128, PART)


def pick_kernel(
    tile_ref, lengths_ref, slots_ref, own_ref, other_hit, picked_ref, rows_s, own_hit
):
    tile = tile_ref[0]
    own_rows(own_ref, rows_s, tile)
    code = slots_ref[...] + 1
    code = jnp.concatenate([code // 16, code % 16] + [jnp.zeros_like(code)] * 6, 0)
    slot = lax.broadcasted_iota(jnp.int32, (SLOTS, SLOTS), 0)
    col = lax.broadcasted_iota(jnp.int32, (1, SLOTS), 1)
    group, place = col // 128, col % 128
    core = (group // PAIRS + tile) % 2
    source = SLOT_DEV * (place // 2) + FR_DEV * core + 2 * (group % PAIRS) + place % 2
    moved = jnp.where(slot == source, 1.0, 0.0).astype(bf16)
    code = jnp.dot(code.astype(f32).astype(bf16), moved, preferred_element_type=f32)
    held = (code[0:1] * 16.0 + code[1:2]).astype(jnp.int32) - 1
    row = lax.broadcasted_iota(jnp.int32, (128, 1), 0)
    for step in range(PAIRS):
        frame = FR_DEV * (row // 2) + 2 * step + row % 2
        first, last = frame < 0, frame + 1 == FRAMES
        start = 0
        for c in range(CLIPS):
            first |= frame == start
            last |= frame + 1 == start
            start += lengths_ref[c]
        wanted = (jnp.where(first, -2, frame - 1), frame, jnp.where(last, -2, frame + 1))
        for tap, want in enumerate(wanted):
            rows = slice((PAIRS * step + tap) * 128, (PAIRS * step + tap + 1) * 128)
            hit = jnp.where(held == want, 1.0, 0.0).astype(bf16)
            own_hit[rows, :] = hit[:, : SLOTS // 2]
            other_hit[rows, :] = hit[:, SLOTS // 2 :]
    picked_ref[...] = jnp.dot(own_hit[...], rows_s[...], preferred_element_type=f32)


def pick(tile, lengths, slots, own):
    smem, vmem = (pl.BlockSpec(memory_space=m) for m in (pltpu.SMEM, pltpu.VMEM))
    return pl.pallas_call(
        pick_kernel,
        in_specs=[smem, smem, vmem, vmem],
        out_specs=[vmem, vmem],
        out_shape=[
            pltpu.VMEM((9 * 128, SLOTS // 2), bf16),
            pltpu.VMEM((9 * 128, PART), f32),
        ],
        scratch_shapes=[
            pltpu.VMEM((SLOTS // 2, PART), bf16),
            pltpu.VMEM((9 * 128, SLOTS // 2), bf16),
        ],
        compiler_params=pltpu.CompilerParams(vmem_limit_bytes=SMALL_VMEM),
        name="pick_own_rows",
    )(tile, lengths, slots, in_vmem(own))


def mix_kernel(tile_ref, other_ref, other_hit, picked_ref, taps_ref, out_ref, rows_s, picked_s):
    tile = tile_ref[0]
    own_rows(other_ref, rows_s, tile)
    picked_s[...] = jnp.dot(other_hit[...], rows_s[...], preferred_element_type=f32)
    taps = taps_ref[:, pl.ds(pl.multiple_of(512 * tile, 128), PART)]
    for step in range(PAIRS):
        mixed = 0.0
        for tap in range(3):
            first = (PAIRS * step + tap) * 128
            rows = slice(first, first + 128)
            mixed += taps[tap : tap + 1] * (picked_s[rows, :] + picked_ref[rows, :])
        mixed = mixed.astype(bf16).reshape(FRAME_DEVS, 2, PART)
        out_ref[:, :, step * PART : (step + 1) * PART] = mixed


def mix(tile, other, other_hit, picked, taps):
    smem, vmem = (pl.BlockSpec(memory_space=m) for m in (pltpu.SMEM, pltpu.VMEM))
    return pl.pallas_call(
        mix_kernel,
        in_specs=[smem, vmem, vmem, vmem, vmem],
        out_specs=vmem,
        out_shape=pltpu.VMEM((FRAME_DEVS, 2, PAIRS * PART), bf16),
        scratch_shapes=[
            pltpu.VMEM((SLOTS // 2, PART), bf16),
            pltpu.VMEM((9 * 128, PART), f32),
        ],
        compiler_params=pltpu.CompilerParams(vmem_limit_bytes=SMALL_VMEM),
        name="mix_rows",
    )(tile, in_vmem(other), in_vmem(other_hit), in_vmem(picked), taps)


def deinterleave(rows):
    row = lax.broadcasted_iota(jnp.int32, (128, 128), 0)
    col = lax.broadcasted_iota(jnp.int32, (128, 128), 1)
    order = jnp.where(col == 2 * (row % BLOCKS) + row // BLOCKS, 1.0, 0.0).astype(bf16)
    return jnp.dot(order, rows, preferred_element_type=f32).astype(bf16)


def project_own_kernel(tile_ref, own_ref, w_ref, part_ref, rows_s):
    for j in range(PAIRS):
        rows = own_ref[:, :, j * PART : (j + 1) * PART].reshape(128, PART)
        rows_s[j * 128 : (j + 1) * 128, :] = deinterleave(rows)
    first = pl.multiple_of(512 * tile_ref[0], 128)
    for lo in range(0, OUT_DEV, 256):
        weights = w_ref[pl.ds(first, PART), lo : lo + 256]
        part_ref[:, lo : lo + 256] = jnp.dot(rows_s[...], weights, preferred_element_type=f32)


def project_own(tile, own, w_proj):
    smem, vmem = (pl.BlockSpec(memory_space=m) for m in (pltpu.SMEM, pltpu.VMEM))
    return pl.pallas_call(
        project_own_kernel,
        in_specs=[smem, vmem, vmem],
        out_specs=vmem,
        out_shape=pltpu.VMEM((FR_DEV * BLOCKS, OUT_DEV), f32),
        scratch_shapes=[pltpu.VMEM((FR_DEV * BLOCKS, PART), bf16)],
        compiler_params=pltpu.CompilerParams(vmem_limit_bytes=SMALL_VMEM),
        name="project_own_channels",
    )(tile, in_vmem(own), in_vmem(w_proj))


def project_kernel(tile_ref, other_ref, part_ref, w_ref, out_hbm, rows_s, out_s, sems):
    tile = tile_ref[0]
    for j in range(PAIRS):
        cols = pl.ds(pl.multiple_of(j * PART + 128 * (1 - tile), 128), REST)
        rows_s[j * 128 : (j + 1) * 128, :] = deinterleave(other_ref[:, :, cols].reshape(128, REST))
    first = pl.multiple_of(PART * (1 - tile), 128)
    copies = []
    for n, lo in enumerate(range(0, OUT_DEV, OUT_CUT)):
        for mid in range(lo, lo + OUT_CUT, 256):
            cols = slice(mid, min(mid + 256, lo + OUT_CUT))
            weights = w_ref[pl.ds(first, REST), cols]
            out = jnp.dot(rows_s[...], weights, preferred_element_type=f32) + part_ref[:, cols]
            out_s[:, :, cols] = out.astype(bf16).reshape(FR_DEV, BLOCKS, cols.stop - cols.start)
        cols = pl.ds(lo, OUT_CUT)
        copies.append(
            pltpu.make_async_copy(out_s.at[:, :, cols], out_hbm.at[:, :, cols], sems.at[n])
        )
        copies[n].start()
    for copy in copies:
        copy.wait()


def project(tile, other, part, w_proj):
    smem, vmem = (pl.BlockSpec(memory_space=m) for m in (pltpu.SMEM, pltpu.VMEM))
    shape = (FR_DEV, BLOCKS, OUT_DEV)
    return pl.pallas_call(
        project_kernel,
        in_specs=[smem, vmem, vmem, vmem],
        out_specs=pl.BlockSpec(memory_space=pltpu.HBM),
        out_shape=jax.ShapeDtypeStruct(shape, bf16),
        scratch_shapes=[
            pltpu.VMEM((FR_DEV * BLOCKS, REST), bf16),
            pltpu.VMEM(shape, bf16),
            pltpu.SemaphoreType.DMA((OUT_DEV // OUT_CUT,)),
        ],
        compiler_params=pltpu.CompilerParams(vmem_limit_bytes=SMALL_VMEM),
        name="project_rows",
    )(tile, in_vmem(other), in_vmem(part), in_vmem(w_proj))


SWAP = [(0, 1), (1, 0)]


def on_device(
    frames_in, norm_gain, norm_bias, w_qkv, w_out, time_taps, w_proj, clip_lengths, frame_slot, block_map
):
    core = jnp.reshape(lax.axis_index("tile"), (1,)).astype(jnp.int32)
    sent = cut_sent(core, frames_in)
    other = lax.ppermute(sent, "tile", SWAP)
    frames_in, _ = lax.optimization_barrier((frames_in, sent))
    own, own_normed, w_qkv, pool = stage(
        core, frames_in, norm_gain, norm_bias, block_map[None], w_qkv
    )
    pooled = encode(
        own, own_normed, other, norm_gain, norm_bias, w_qkv, w_out, pool
    )
    spread = lax.all_to_all(pooled, "frame", split_axis=0, concat_axis=0, tiled=True)
    spread_other = lax.ppermute(spread, "tile", SWAP)
    other_hit, picked = pick(core, clip_lengths, frame_slot[None], spread)
    mixed = mix(core, spread_other, other_hit, picked, time_taps)
    home = lax.all_to_all(mixed, "frame", split_axis=0, concat_axis=0, tiled=True)
    home_other = lax.ppermute(home, "tile", SWAP)
    part = project_own(core, home, w_proj)
    return project(core, home_other, part, w_proj)


def solution(mesh):
    in_specs = (P("frame", "tile", None), P(), P(), P(), P(), P(), P(None, "tile"), P(), P(), P())
    return jax.shard_map(
        on_device, mesh=mesh, in_specs=in_specs, out_specs=P("frame", None, "tile"), check_vma=False
    )
```

```python
import math

import jax
import jax.numpy as jnp
from jax import lax
from jax.experimental import pallas as pl
from jax.experimental.pallas import tpu as pltpu
from jax.sharding import PartitionSpec as P

D = 1152
HEADS = 16
HEAD_DIM = 72
PATCH = 256
HALF = 128
BLOCKS = 64
FRAMES = 384
FRAME_DEVS = 64
CLIPS = 6
FR_DEV = 6
SLOT_DEV = 12
SLOTS = 768
PAIRS = 3
PIECES = 9
PART = 640
REST = 512
OUT_CUTS = (0, 512, 1024, 1536, 1792)
OUT_DEV = 1792
NORM_EPS = 1e-6
SCORE_SCALE = math.log2(math.e) / math.sqrt(HEAD_DIM)
STAGE_VMEM = 16 << 20
ENCODE_VMEM = 34 << 20
SMALL_VMEM = 16 << 20

bf16 = jnp.bfloat16
f32 = jnp.float32
NT = (((1,), (1,)), ((), ()))


def head_lanes(head):
    first, last = HEAD_DIM * head, HEAD_DIM * (head + 1) - 1
    return first // 128 * 128, (last // 128 + 1) * 128


def in_vmem(x):
    return pltpu.with_memory_space_constraint(x, pltpu.VMEM)


def in_hbm(x):
    return pltpu.with_memory_space_constraint(x, pltpu.HBM)


def normalise(rows, gain_ref, bias_ref):
    gain, bias = gain_ref[...].reshape(1, D), bias_ref[...].reshape(1, D)
    rows = rows.astype(f32)
    centred = rows - jnp.sum(rows, -1, keepdims=True) * (1.0 / D)
    variance = jnp.sum(centred * centred, -1, keepdims=True) * (1.0 / D)
    return (centred * lax.rsqrt(variance + NORM_EPS) * gain + bias).astype(bf16)


def cut_kernel(tile_ref, frames_hbm, out_ref, sems):
    first = FR_DEV * (1 - tile_ref[0])
    copies = []
    for f in range(FR_DEV):
        copies.append(
            pltpu.make_async_copy(frames_hbm.at[first + f], out_ref.at[f], sems.at[f])
        )
        copies[f].start()
    for copy in copies:
        copy.wait()


def cut_sent(tile, frames_in):
    return pl.pallas_call(
        cut_kernel,
        in_specs=[pl.BlockSpec(memory_space=m) for m in (pltpu.SMEM, pltpu.HBM)],
        out_specs=pl.BlockSpec(memory_space=pltpu.VMEM),
        out_shape=pltpu.VMEM((FR_DEV, HALF, D), bf16),
        scratch_shapes=[pltpu.SemaphoreType.DMA((FR_DEV,))],
        compiler_params=pltpu.CompilerParams(vmem_limit_bytes=STAGE_VMEM),
        name="cut_sent_half",
    )(tile, in_hbm(frames_in))


def stage_kernel(
    tile_ref, frames_hbm, gain_ref, bias_ref, map_ref, wqkv_hbm,
    own_ref, normed_ref, wqkv_ref, pool_ref, sems,
):
    rows = pl.ds(FR_DEV * tile_ref[0], FR_DEV)
    copies = [pltpu.make_async_copy(frames_hbm.at[rows], own_ref, sems.at[0])]
    step = D // PIECES
    for n in range(PIECES):
        part = pl.ds(n * step, step)
        copies.append(pltpu.make_async_copy(wqkv_hbm.at[part], wqkv_ref.at[part], sems.at[n + 1]))
    for copy in copies:
        copy.start()
    pool_ref[...] = pooling(tile_ref[0], map_ref)
    copies[0].wait()
    for f in range(FR_DEV):
        normed_ref[f] = normalise(own_ref[f], gain_ref, bias_ref)
    for copy in copies[1:]:
        copy.wait()


def stage(tile, frames_in, gain, bias, block_map, w_qkv):
    smem, vmem, hbm = (pl.BlockSpec(memory_space=m) for m in (pltpu.SMEM, pltpu.VMEM, pltpu.HBM))
    return pl.pallas_call(
        stage_kernel,
        in_specs=[smem, hbm, vmem, vmem, vmem, hbm],
        out_specs=[vmem] * 4,
        out_shape=[
            pltpu.VMEM((FR_DEV, HALF, D), bf16),
            pltpu.VMEM((FR_DEV, HALF, D), bf16),
            pltpu.VMEM((D, 3 * D), bf16),
            pltpu.VMEM((2 * BLOCKS, 2 * PATCH), bf16),
        ],
        scratch_shapes=[pltpu.SemaphoreType.DMA((1 + PIECES,))],
        compiler_params=pltpu.CompilerParams(vmem_limit_bytes=STAGE_VMEM),
        name="stage_operands",
    )(tile, in_hbm(frames_in), gain, bias, block_map, in_hbm(w_qkv))


def project_qkv(normed_s, w_ref, qk_s, vt_s):
    starts = list(range(2 * D, 3 * D, 256)) + [0, 1024, 256, 1280, 512, 1536, 768, 1792, 2048]
    for lo in starts:
        hi = min(lo + 256, 3 * D)
        part = jnp.dot(normed_s[...], w_ref[:, lo:hi], preferred_element_type=f32)
        if hi <= 2 * D:
            qk_s[:, lo:hi] = part.astype(bf16)
        else:
            vt_s[lo - 2 * D : hi - 2 * D, :] = part.astype(bf16).T


def attend(qk_s, vt_s, ctx_s):
    lane = lax.broadcasted_iota(jnp.int32, (1, D), 1)
    ones = jnp.ones((16, PATCH), bf16)

    def scores(s, head):
        lo, hi = head_lanes(head)
        start = HEAD_DIM * head
        mine = (lane[:, lo:hi] >= start) & (lane[:, lo:hi] < start + HEAD_DIM)
        rows = slice(s * PATCH, (s + 1) * PATCH)
        keys = qk_s[rows, D + lo : D + hi]
        keys = jnp.where(mine, keys, jnp.zeros_like(keys))
        return lax.dot_general(keys, qk_s[rows, lo:hi], NT, preferred_element_type=f32)

    def weigh(score):
        top = jnp.max(score, 0, keepdims=True)
        return jnp.exp2((score - top) * SCORE_SCALE).astype(bf16)

    def total(s, head, weights):
        skip = 8 * (head % 2)
        first = HEAD_DIM * head - skip
        cols = slice(s * PATCH, (s + 1) * PATCH)
        values = jnp.concatenate([vt_s[first : first + 80, cols], ones], 0)
        summed = jnp.dot(values, weights, preferred_element_type=f32)
        ctx_s[HEAD_DIM * head : HEAD_DIM * (head + 1), cols] = (
            summed[skip : skip + HEAD_DIM] / summed[80:81]
        )

    items = [(s, head) for s in range(2) for head in range(HEADS)]
    score, weights = {}, {}
    for n in range(-6, len(items)):
        if n + 6 < len(items):
            score[n + 6] = scores(*items[n + 6])
        if 0 <= n + 3 < len(items):
            weights[n + 3] = weigh(score.pop(n + 3))
        if n >= 0:
            total(*items[n], weights.pop(n))


def pooling(tile, map_ref):
    block = lax.broadcasted_iota(jnp.int32, (BLOCKS, 2 * PATCH), 0)
    col = lax.broadcasted_iota(jnp.int32, (BLOCKS, 2 * PATCH), 1)
    col_block = (col % HALF) // 4 + BLOCKS // 2 * ((col // HALF + tile) % 2)
    row = lax.broadcasted_iota(jnp.int32, (2 * BLOCKS, 1), 0)
    placing = jnp.where(map_ref[...] == row // 2, 1.0, 0.0).astype(bf16)
    member = jnp.where(block == col_block, 0.25, 0.0).astype(bf16)
    member = jnp.dot(placing, member, preferred_element_type=f32)
    frame_of = lax.broadcasted_iota(jnp.int32, (1, 2 * PATCH), 1) // PATCH
    return jnp.where(frame_of == row % 2, member, 0.0).astype(bf16)


def encode_kernel(
    own_ref, own_normed, other_ref, gain_ref, bias_ref, wqkv_ref, wout_hbm, pool_ref, out_ref,
    wout_s, normed_s, qk_s, vt_s, ctx_s, pooled_x, pooled_ctx, sem,
):
    wout_copy = pltpu.make_async_copy(wout_hbm, wout_s, sem)
    wout_copy.start()

    def one_pair(pair, carry):
        for s in range(2):
            frame = 2 * pair + s
            mid = s * PATCH + HALF
            normed_s[s * PATCH : mid, :] = own_normed[frame]
            normed_s[mid : (s + 1) * PATCH, :] = normalise(other_ref[frame], gain_ref, bias_ref)
        project_qkv(normed_s, wqkv_ref, qk_s, vt_s)
        attend(qk_s, vt_s, ctx_s)
        rows = pl.ds(pl.multiple_of(pair * 2 * BLOCKS, 2 * BLOCKS), 2 * BLOCKS)
        pooled = lax.dot_general(
            pool_ref[...], ctx_s[...].astype(bf16), NT, preferred_element_type=f32
        )
        pooled_ctx[rows, :] = pooled.astype(bf16)
        patches = [ref[2 * pair + s] for s in range(2) for ref in (own_ref, other_ref)]
        patches = jnp.concatenate(patches, 0)
        pooled_x[rows, :] = jnp.dot(pool_ref[...], patches, preferred_element_type=f32)
        return carry

    lax.fori_loop(0, PAIRS, one_pair, 0)
    wout_copy.wait()
    for pair in range(PAIRS):
        rows = slice(pair * 2 * BLOCKS, (pair + 1) * 2 * BLOCKS)
        total = jnp.dot(pooled_ctx[rows, :], wout_s[...], preferred_element_type=f32)
        total = (total + pooled_x[rows, :]).astype(bf16)
        out_ref[:, :, pair * D : (pair + 1) * D] = total.reshape(BLOCKS, 2, D)


def encode(own, own_normed, other, gain, bias, w_qkv, w_out, pool):
    vmem, hbm = (pl.BlockSpec(memory_space=m) for m in (pltpu.VMEM, pltpu.HBM))
    return pl.pallas_call(
        encode_kernel,
        in_specs=[vmem] * 6 + [hbm, vmem],
        out_specs=vmem,
        out_shape=pltpu.VMEM((BLOCKS, 2, PAIRS * D), bf16),
        scratch_shapes=[
            pltpu.VMEM((D, D), bf16),
            pltpu.VMEM((2 * PATCH, D), bf16),
            pltpu.VMEM((2 * PATCH, 2 * D), bf16),
            pltpu.VMEM((D, 2 * PATCH), bf16),
            pltpu.VMEM((D, 2 * PATCH), f32),
            pltpu.VMEM((PAIRS * 2 * BLOCKS, D), f32),
            pltpu.VMEM((PAIRS * 2 * BLOCKS, D), bf16),
            pltpu.SemaphoreType.DMA,
        ],
        compiler_params=pltpu.CompilerParams(vmem_limit_bytes=ENCODE_VMEM),
        name="encode_frames",
    )(
        in_vmem(own), in_vmem(own_normed), in_vmem(other), gain, bias,
        in_vmem(w_qkv), in_hbm(w_out), in_vmem(pool),
    )


def own_rows(ref, rows_s, tile):
    for j in range(PAIRS):
        cols = pl.ds(pl.multiple_of(j * D + 512 * tile, 128), PART)
        rows_s[j * 128 : (j + 1) * 128, :] = ref[:, :, cols].reshape(128, PART)


def pick_kernel(
    tile_ref, lengths_ref, slots_ref, own_ref, other_hit, picked_ref, rows_s, own_hit
):
    tile = tile_ref[0]
    own_rows(own_ref, rows_s, tile)
    code = slots_ref[...] + 1
    code = jnp.concatenate([code // 16, code % 16] + [jnp.zeros_like(code)] * 6, 0)
    slot = lax.broadcasted_iota(jnp.int32, (SLOTS, SLOTS), 0)
    col = lax.broadcasted_iota(jnp.int32, (1, SLOTS), 1)
    group, place = col // 128, col % 128
    core = (group // PAIRS + tile) % 2
    source = SLOT_DEV * (place // 2) + FR_DEV * core + 2 * (group % PAIRS) + place % 2
    moved = jnp.where(slot == source, 1.0, 0.0).astype(bf16)
    code = jnp.dot(code.astype(f32).astype(bf16), moved, preferred_element_type=f32)
    held = (code[0:1] * 16.0 + code[1:2]).astype(jnp.int32) - 1
    row = lax.broadcasted_iota(jnp.int32, (128, 1), 0)
    for step in range(PAIRS):
        frame = FR_DEV * (row // 2) + 2 * step + row % 2
        first, last = frame < 0, frame + 1 == FRAMES
        start = 0
        for c in range(CLIPS):
            first |= frame == start
            last |= frame + 1 == start
            start += lengths_ref[c]
        wanted = (jnp.where(first, -2, frame - 1), frame, jnp.where(last, -2, frame + 1))
        for tap, want in enumerate(wanted):
            rows = slice((PAIRS * step + tap) * 128, (PAIRS * step + tap + 1) * 128)
            hit = jnp.where(held == want, 1.0, 0.0).astype(bf16)
            own_hit[rows, :] = hit[:, : SLOTS // 2]
            other_hit[rows, :] = hit[:, SLOTS // 2 :]
    picked_ref[...] = jnp.dot(own_hit[...], rows_s[...], preferred_element_type=f32)


def pick(tile, lengths, slots, own):
    smem, vmem = (pl.BlockSpec(memory_space=m) for m in (pltpu.SMEM, pltpu.VMEM))
    return pl.pallas_call(
        pick_kernel,
        in_specs=[smem, smem, vmem, vmem],
        out_specs=[vmem, vmem],
        out_shape=[
            pltpu.VMEM((9 * 128, SLOTS // 2), bf16),
            pltpu.VMEM((9 * 128, PART), f32),
        ],
        scratch_shapes=[
            pltpu.VMEM((SLOTS // 2, PART), bf16),
            pltpu.VMEM((9 * 128, SLOTS // 2), bf16),
        ],
        compiler_params=pltpu.CompilerParams(vmem_limit_bytes=SMALL_VMEM),
        name="pick_own_rows",
    )(tile, lengths, slots, in_vmem(own))


def mix_kernel(tile_ref, other_ref, other_hit, picked_ref, taps_ref, out_ref, rows_s, picked_s):
    tile = tile_ref[0]
    own_rows(other_ref, rows_s, tile)
    picked_s[...] = jnp.dot(other_hit[...], rows_s[...], preferred_element_type=f32)
    taps = taps_ref[:, pl.ds(pl.multiple_of(512 * tile, 128), PART)]
    for step in range(PAIRS):
        mixed = 0.0
        for tap in range(3):
            first = (PAIRS * step + tap) * 128
            rows = slice(first, first + 128)
            mixed += taps[tap : tap + 1] * (picked_s[rows, :] + picked_ref[rows, :])
        mixed = mixed.astype(bf16).reshape(FRAME_DEVS, 2, PART)
        out_ref[:, :, step * PART : (step + 1) * PART] = mixed


def mix(tile, other, other_hit, picked, taps):
    smem, vmem = (pl.BlockSpec(memory_space=m) for m in (pltpu.SMEM, pltpu.VMEM))
    return pl.pallas_call(
        mix_kernel,
        in_specs=[smem, vmem, vmem, vmem, vmem],
        out_specs=vmem,
        out_shape=pltpu.VMEM((FRAME_DEVS, 2, PAIRS * PART), bf16),
        scratch_shapes=[
            pltpu.VMEM((SLOTS // 2, PART), bf16),
            pltpu.VMEM((9 * 128, PART), f32),
        ],
        compiler_params=pltpu.CompilerParams(vmem_limit_bytes=SMALL_VMEM),
        name="mix_rows",
    )(tile, in_vmem(other), in_vmem(other_hit), in_vmem(picked), taps)


def deinterleave(rows):
    row = lax.broadcasted_iota(jnp.int32, (128, 128), 0)
    col = lax.broadcasted_iota(jnp.int32, (128, 128), 1)
    order = jnp.where(col == 2 * (row % BLOCKS) + row // BLOCKS, 1.0, 0.0).astype(bf16)
    return jnp.dot(order, rows, preferred_element_type=f32).astype(bf16)


def project_own_kernel(tile_ref, own_ref, w_ref, part_ref, rows_s):
    for j in range(PAIRS):
        rows = own_ref[:, :, j * PART : (j + 1) * PART].reshape(128, PART)
        rows_s[j * 128 : (j + 1) * 128, :] = deinterleave(rows)
    first = pl.multiple_of(512 * tile_ref[0], 128)
    for lo in range(0, OUT_DEV, 256):
        weights = w_ref[pl.ds(first, PART), lo : lo + 256]
        part_ref[:, lo : lo + 256] = jnp.dot(rows_s[...], weights, preferred_element_type=f32)


def project_own(tile, own, w_proj):
    smem, vmem = (pl.BlockSpec(memory_space=m) for m in (pltpu.SMEM, pltpu.VMEM))
    return pl.pallas_call(
        project_own_kernel,
        in_specs=[smem, vmem, vmem],
        out_specs=vmem,
        out_shape=pltpu.VMEM((FR_DEV * BLOCKS, OUT_DEV), f32),
        scratch_shapes=[pltpu.VMEM((FR_DEV * BLOCKS, PART), bf16)],
        compiler_params=pltpu.CompilerParams(vmem_limit_bytes=SMALL_VMEM),
        name="project_own_channels",
    )(tile, in_vmem(own), in_vmem(w_proj))


def project_kernel(tile_ref, other_ref, part_ref, w_ref, out_hbm, rows_s, out_s, sems):
    tile = tile_ref[0]
    for j in range(PAIRS):
        cols = pl.ds(pl.multiple_of(j * PART + 128 * (1 - tile), 128), REST)
        rows_s[j * 128 : (j + 1) * 128, :] = deinterleave(other_ref[:, :, cols].reshape(128, REST))
    first = pl.multiple_of(PART * (1 - tile), 128)
    copies = []
    for n, (lo, hi) in enumerate(zip(OUT_CUTS[:-1], OUT_CUTS[1:])):
        for mid in range(lo, hi, 256):
            cols = slice(mid, mid + 256)
            weights = w_ref[pl.ds(first, REST), cols]
            out = jnp.dot(rows_s[...], weights, preferred_element_type=f32) + part_ref[:, cols]
            out_s[:, :, cols] = out.astype(bf16).reshape(FR_DEV, BLOCKS, 256)
        cols = pl.ds(lo, hi - lo)
        copies.append(
            pltpu.make_async_copy(out_s.at[:, :, cols], out_hbm.at[:, :, cols], sems.at[n])
        )
        copies[n].start()
    for copy in copies:
        copy.wait()


def project(tile, other, part, w_proj):
    smem, vmem = (pl.BlockSpec(memory_space=m) for m in (pltpu.SMEM, pltpu.VMEM))
    shape = (FR_DEV, BLOCKS, OUT_DEV)
    return pl.pallas_call(
        project_kernel,
        in_specs=[smem, vmem, vmem, vmem],
        out_specs=pl.BlockSpec(memory_space=pltpu.HBM),
        out_shape=jax.ShapeDtypeStruct(shape, bf16),
        scratch_shapes=[
            pltpu.VMEM((FR_DEV * BLOCKS, REST), bf16),
            pltpu.VMEM(shape, bf16),
            pltpu.SemaphoreType.DMA((len(OUT_CUTS) - 1,)),
        ],
        compiler_params=pltpu.CompilerParams(vmem_limit_bytes=SMALL_VMEM),
        name="project_rows",
    )(tile, in_vmem(other), in_vmem(part), in_vmem(w_proj))


SWAP = [(0, 1), (1, 0)]


def on_device(
    frames_in, norm_gain, norm_bias, w_qkv, w_out, time_taps, w_proj, clip_lengths, frame_slot, block_map
):
    core = jnp.reshape(lax.axis_index("tile"), (1,)).astype(jnp.int32)
    sent = cut_sent(core, frames_in)
    other = lax.ppermute(sent, "tile", SWAP)
    frames_in, _ = lax.optimization_barrier((frames_in, sent))
    own, own_normed, w_qkv, pool = stage(
        core, frames_in, norm_gain, norm_bias, block_map[None], w_qkv
    )
    pooled = encode(
        own, own_normed, other, norm_gain, norm_bias, w_qkv, w_out, pool
    )
    spread = lax.all_to_all(pooled, "frame", split_axis=0, concat_axis=0, tiled=True)
    spread_other = lax.ppermute(spread, "tile", SWAP)
    other_hit, picked = pick(core, clip_lengths, frame_slot[None], spread)
    mixed = mix(core, spread_other, other_hit, picked, time_taps)
    home = lax.all_to_all(mixed, "frame", split_axis=0, concat_axis=0, tiled=True)
    home_other = lax.ppermute(home, "tile", SWAP)
    part = project_own(core, home, w_proj)
    return project(core, home_other, part, w_proj)


def solution(mesh):
    in_specs = (P("frame", "tile", None), P(), P(), P(), P(), P(), P(None, "tile"), P(), P(), P())
    return jax.shard_map(
        on_device, mesh=mesh, in_specs=in_specs, out_specs=P("frame", None, "tile"), check_vma=False
    )
```

```python
import math

import jax
import jax.numpy as jnp
from jax import lax
from jax.experimental import pallas as pl
from jax.experimental.pallas import tpu as pltpu
from jax.sharding import PartitionSpec as P

D = 1152
HEADS = 16
HEAD_DIM = 72
PATCH = 256
HALF = 128
BLOCKS = 64
FRAMES = 384
FRAME_DEVS = 64
CLIPS = 6
FR_DEV = 6
SLOT_DEV = 12
SLOTS = 768
PAIRS = 3
PIECES = 9
PART = 640
REST = 512
OUT_CUTS = (0, 512, 1024, 1536, 1792)
OUT_DEV = 1792
NORM_EPS = 1e-6
SCORE_SCALE = math.log2(math.e) / math.sqrt(HEAD_DIM)
STAGE_VMEM = 16 << 20
ENCODE_VMEM = 34 << 20
SMALL_VMEM = 16 << 20

bf16 = jnp.bfloat16
f32 = jnp.float32
NT = (((1,), (1,)), ((), ()))


def head_lanes(head):
    first, last = HEAD_DIM * head, HEAD_DIM * (head + 1) - 1
    return first // 128 * 128, (last // 128 + 1) * 128


def in_vmem(x):
    return pltpu.with_memory_space_constraint(x, pltpu.VMEM)


def in_hbm(x):
    return pltpu.with_memory_space_constraint(x, pltpu.HBM)


def normalise(rows, gain_ref, bias_ref):
    gain, bias = gain_ref[...].reshape(1, D), bias_ref[...].reshape(1, D)
    rows = rows.astype(f32)
    centred = rows - jnp.sum(rows, -1, keepdims=True) * (1.0 / D)
    variance = jnp.sum(centred * centred, -1, keepdims=True) * (1.0 / D)
    return (centred * lax.rsqrt(variance + NORM_EPS) * gain + bias).astype(bf16)


def cut_kernel(tile_ref, frames_hbm, out_ref, sems):
    first = FR_DEV * (1 - tile_ref[0])
    copies = []
    for f in range(FR_DEV):
        copies.append(
            pltpu.make_async_copy(frames_hbm.at[first + f], out_ref.at[f], sems.at[f])
        )
        copies[f].start()
    for copy in copies:
        copy.wait()


def cut_sent(tile, frames_in):
    return pl.pallas_call(
        cut_kernel,
        in_specs=[pl.BlockSpec(memory_space=m) for m in (pltpu.SMEM, pltpu.HBM)],
        out_specs=pl.BlockSpec(memory_space=pltpu.VMEM),
        out_shape=pltpu.VMEM((FR_DEV, HALF, D), bf16),
        scratch_shapes=[pltpu.SemaphoreType.DMA((FR_DEV,))],
        compiler_params=pltpu.CompilerParams(vmem_limit_bytes=STAGE_VMEM),
        name="cut_sent_half",
    )(tile, in_hbm(frames_in))


def stage_kernel(
    tile_ref, frames_hbm, gain_ref, bias_ref, map_ref, wqkv_hbm,
    own_ref, normed_ref, wqkv_ref, pool_ref, sems,
):
    rows = pl.ds(FR_DEV * tile_ref[0], FR_DEV)
    copies = [pltpu.make_async_copy(frames_hbm.at[rows], own_ref, sems.at[0])]
    step = D // PIECES
    for n in range(PIECES):
        part = pl.ds(n * step, step)
        copies.append(pltpu.make_async_copy(wqkv_hbm.at[part], wqkv_ref.at[part], sems.at[n + 1]))
    for copy in copies:
        copy.start()
    pool_ref[...] = pooling(tile_ref[0], map_ref)
    copies[0].wait()
    for f in range(FR_DEV):
        normed_ref[f] = normalise(own_ref[f], gain_ref, bias_ref)
    for copy in copies[1:]:
        copy.wait()


def stage(tile, frames_in, gain, bias, block_map, w_qkv):
    smem, vmem, hbm = (pl.BlockSpec(memory_space=m) for m in (pltpu.SMEM, pltpu.VMEM, pltpu.HBM))
    return pl.pallas_call(
        stage_kernel,
        in_specs=[smem, hbm, vmem, vmem, vmem, hbm],
        out_specs=[vmem] * 4,
        out_shape=[
            pltpu.VMEM((FR_DEV, HALF, D), bf16),
            pltpu.VMEM((FR_DEV, HALF, D), bf16),
            pltpu.VMEM((D, 3 * D), bf16),
            pltpu.VMEM((2 * BLOCKS, 2 * PATCH), bf16),
        ],
        scratch_shapes=[pltpu.SemaphoreType.DMA((1 + PIECES,))],
        compiler_params=pltpu.CompilerParams(vmem_limit_bytes=STAGE_VMEM),
        name="stage_operands",
    )(tile, in_hbm(frames_in), gain, bias, block_map, in_hbm(w_qkv))


def project_qkv(normed_s, w_ref, qk_s, vt_s):
    starts = list(range(2 * D, 3 * D, 256)) + [0, 1024, 256, 1280, 512, 1536, 768, 1792, 2048]
    for lo in starts:
        hi = min(lo + 256, 3 * D)
        part = jnp.dot(normed_s[...], w_ref[:, lo:hi], preferred_element_type=f32)
        if hi <= 2 * D:
            qk_s[:, lo:hi] = part.astype(bf16)
        else:
            vt_s[lo - 2 * D : hi - 2 * D, :] = part.astype(bf16).T


def attend(qk_s, vt_s, ctx_s):
    lane = lax.broadcasted_iota(jnp.int32, (1, D), 1)
    ones = jnp.ones((16, PATCH), bf16)

    def scores(s, head):
        lo, hi = head_lanes(head)
        start = HEAD_DIM * head
        mine = (lane[:, lo:hi] >= start) & (lane[:, lo:hi] < start + HEAD_DIM)
        rows = slice(s * PATCH, (s + 1) * PATCH)
        keys = qk_s[rows, D + lo : D + hi]
        keys = jnp.where(mine, keys, jnp.zeros_like(keys))
        return lax.dot_general(keys, qk_s[rows, lo:hi], NT, preferred_element_type=f32)

    def weigh(score):
        top = jnp.max(score, 0, keepdims=True)
        return jnp.exp2((score - top) * SCORE_SCALE).astype(bf16)

    def total(s, head, weights):
        skip = 8 * (head % 2)
        first = HEAD_DIM * head - skip
        cols = slice(s * PATCH, (s + 1) * PATCH)
        values = jnp.concatenate([vt_s[first : first + 80, cols], ones], 0)
        summed = jnp.dot(values, weights, preferred_element_type=f32)
        ctx_s[HEAD_DIM * head : HEAD_DIM * (head + 1), cols] = (
            summed[skip : skip + HEAD_DIM] / summed[80:81]
        )

    items = [(s, head) for s in range(2) for head in range(HEADS)]
    score, weights = {}, {}
    for n in range(-6, len(items)):
        if 0 <= n + 3 < len(items):
            weights[n + 3] = weigh(score.pop(n + 3))
        if 0 <= n + 6 < len(items):
            score[n + 6] = scores(*items[n + 6])
        if n >= 0:
            total(*items[n], weights.pop(n))


def pooling(tile, map_ref):
    block = lax.broadcasted_iota(jnp.int32, (BLOCKS, 2 * PATCH), 0)
    col = lax.broadcasted_iota(jnp.int32, (BLOCKS, 2 * PATCH), 1)
    col_block = (col % HALF) // 4 + BLOCKS // 2 * ((col // HALF + tile) % 2)
    row = lax.broadcasted_iota(jnp.int32, (2 * BLOCKS, 1), 0)
    placing = jnp.where(map_ref[...] == row // 2, 1.0, 0.0).astype(bf16)
    member = jnp.where(block == col_block, 0.25, 0.0).astype(bf16)
    member = jnp.dot(placing, member, preferred_element_type=f32)
    frame_of = lax.broadcasted_iota(jnp.int32, (1, 2 * PATCH), 1) // PATCH
    return jnp.where(frame_of == row % 2, member, 0.0).astype(bf16)


def encode_kernel(
    own_ref, own_normed, other_ref, gain_ref, bias_ref, wqkv_ref, wout_hbm, pool_ref, out_ref,
    wout_s, normed_s, qk_s, vt_s, ctx_s, pooled_x, pooled_ctx, sem,
):
    wout_copy = pltpu.make_async_copy(wout_hbm, wout_s, sem)
    wout_copy.start()

    def one_pair(pair, carry):
        for s in range(2):
            frame = 2 * pair + s
            mid = s * PATCH + HALF
            normed_s[s * PATCH : mid, :] = own_normed[frame]
            normed_s[mid : (s + 1) * PATCH, :] = normalise(other_ref[frame], gain_ref, bias_ref)
        project_qkv(normed_s, wqkv_ref, qk_s, vt_s)
        attend(qk_s, vt_s, ctx_s)
        rows = pl.ds(pl.multiple_of(pair * 2 * BLOCKS, 2 * BLOCKS), 2 * BLOCKS)
        pooled = lax.dot_general(
            pool_ref[...], ctx_s[...].astype(bf16), NT, preferred_element_type=f32
        )
        pooled_ctx[rows, :] = pooled.astype(bf16)
        patches = [ref[2 * pair + s] for s in range(2) for ref in (own_ref, other_ref)]
        patches = jnp.concatenate(patches, 0)
        pooled_x[rows, :] = jnp.dot(pool_ref[...], patches, preferred_element_type=f32)
        return carry

    lax.fori_loop(0, PAIRS, one_pair, 0)
    wout_copy.wait()
    for pair in range(PAIRS):
        rows = slice(pair * 2 * BLOCKS, (pair + 1) * 2 * BLOCKS)
        total = jnp.dot(pooled_ctx[rows, :], wout_s[...], preferred_element_type=f32)
        total = (total + pooled_x[rows, :]).astype(bf16)
        out_ref[:, :, pair * D : (pair + 1) * D] = total.reshape(BLOCKS, 2, D)


def encode(own, own_normed, other, gain, bias, w_qkv, w_out, pool):
    vmem, hbm = (pl.BlockSpec(memory_space=m) for m in (pltpu.VMEM, pltpu.HBM))
    return pl.pallas_call(
        encode_kernel,
        in_specs=[vmem] * 6 + [hbm, vmem],
        out_specs=vmem,
        out_shape=pltpu.VMEM((BLOCKS, 2, PAIRS * D), bf16),
        scratch_shapes=[
            pltpu.VMEM((D, D), bf16),
            pltpu.VMEM((2 * PATCH, D), bf16),
            pltpu.VMEM((2 * PATCH, 2 * D), bf16),
            pltpu.VMEM((D, 2 * PATCH), bf16),
            pltpu.VMEM((D, 2 * PATCH), f32),
            pltpu.VMEM((PAIRS * 2 * BLOCKS, D), f32),
            pltpu.VMEM((PAIRS * 2 * BLOCKS, D), bf16),
            pltpu.SemaphoreType.DMA,
        ],
        compiler_params=pltpu.CompilerParams(vmem_limit_bytes=ENCODE_VMEM),
        name="encode_frames",
    )(
        in_vmem(own), in_vmem(own_normed), in_vmem(other), gain, bias,
        in_vmem(w_qkv), in_hbm(w_out), in_vmem(pool),
    )


def own_rows(ref, rows_s, tile):
    for j in range(PAIRS):
        cols = pl.ds(pl.multiple_of(j * D + 512 * tile, 128), PART)
        rows_s[j * 128 : (j + 1) * 128, :] = ref[:, :, cols].reshape(128, PART)


def tap_sum(picked, taps, step):
    total = 0.0
    for tap in range(3):
        first = (PAIRS * step + tap) * 128
        total += taps[tap : tap + 1] * picked[first : first + 128, :]
    return total


def pick_kernel(
    tile_ref, lengths_ref, slots_ref, own_ref, taps_ref, other_hit, mixed_ref,
    rows_s, own_hit, picked_s,
):
    tile = tile_ref[0]
    own_rows(own_ref, rows_s, tile)
    code = slots_ref[...] + 1
    code = jnp.concatenate([code // 16, code % 16] + [jnp.zeros_like(code)] * 6, 0)
    slot = lax.broadcasted_iota(jnp.int32, (SLOTS, SLOTS), 0)
    col = lax.broadcasted_iota(jnp.int32, (1, SLOTS), 1)
    group, place = col // 128, col % 128
    core = (group // PAIRS + tile) % 2
    source = SLOT_DEV * (place // 2) + FR_DEV * core + 2 * (group % PAIRS) + place % 2
    moved = jnp.where(slot == source, 1.0, 0.0).astype(bf16)
    code = jnp.dot(code.astype(f32).astype(bf16), moved, preferred_element_type=f32)
    held = (code[0:1] * 16.0 + code[1:2]).astype(jnp.int32) - 1
    row = lax.broadcasted_iota(jnp.int32, (128, 1), 0)
    for step in range(PAIRS):
        frame = FR_DEV * (row // 2) + 2 * step + row % 2
        first, last = frame < 0, frame + 1 == FRAMES
        start = 0
        for c in range(CLIPS):
            first |= frame == start
            last |= frame + 1 == start
            start += lengths_ref[c]
        wanted = (jnp.where(first, -2, frame - 1), frame, jnp.where(last, -2, frame + 1))
        for tap, want in enumerate(wanted):
            rows = slice((PAIRS * step + tap) * 128, (PAIRS * step + tap + 1) * 128)
            hit = jnp.where(held == want, 1.0, 0.0).astype(bf16)
            own_hit[rows, :] = hit[:, : SLOTS // 2]
            other_hit[rows, :] = hit[:, SLOTS // 2 :]
    picked_s[...] = jnp.dot(own_hit[...], rows_s[...], preferred_element_type=f32)
    taps = taps_ref[:, pl.ds(pl.multiple_of(512 * tile, 128), PART)]
    for step in range(PAIRS):
        mixed_ref[step * 128 : (step + 1) * 128, :] = tap_sum(picked_s, taps, step)


def pick(tile, lengths, slots, own, taps):
    smem, vmem = (pl.BlockSpec(memory_space=m) for m in (pltpu.SMEM, pltpu.VMEM))
    return pl.pallas_call(
        pick_kernel,
        in_specs=[smem, smem, vmem, vmem, vmem],
        out_specs=[vmem, vmem],
        out_shape=[
            pltpu.VMEM((9 * 128, SLOTS // 2), bf16),
            pltpu.VMEM((PAIRS * 128, PART), f32),
        ],
        scratch_shapes=[
            pltpu.VMEM((SLOTS // 2, PART), bf16),
            pltpu.VMEM((9 * 128, SLOTS // 2), bf16),
            pltpu.VMEM((9 * 128, PART), f32),
        ],
        compiler_params=pltpu.CompilerParams(vmem_limit_bytes=SMALL_VMEM),
        name="pick_own_rows",
    )(tile, lengths, slots, in_vmem(own), taps)


def mix_kernel(tile_ref, other_ref, other_hit, own_mixed, taps_ref, out_ref, rows_s, picked_s):
    tile = tile_ref[0]
    own_rows(other_ref, rows_s, tile)
    picked_s[...] = jnp.dot(other_hit[...], rows_s[...], preferred_element_type=f32)
    taps = taps_ref[:, pl.ds(pl.multiple_of(512 * tile, 128), PART)]
    for step in range(PAIRS):
        mixed = own_mixed[step * 128 : (step + 1) * 128, :] + tap_sum(picked_s, taps, step)
        mixed = mixed.astype(bf16).reshape(FRAME_DEVS, 2, PART)
        out_ref[:, :, step * PART : (step + 1) * PART] = mixed


def mix(tile, other, other_hit, own_mixed, taps):
    smem, vmem = (pl.BlockSpec(memory_space=m) for m in (pltpu.SMEM, pltpu.VMEM))
    return pl.pallas_call(
        mix_kernel,
        in_specs=[smem, vmem, vmem, vmem, vmem],
        out_specs=vmem,
        out_shape=pltpu.VMEM((FRAME_DEVS, 2, PAIRS * PART), bf16),
        scratch_shapes=[
            pltpu.VMEM((SLOTS // 2, PART), bf16),
            pltpu.VMEM((9 * 128, PART), f32),
        ],
        compiler_params=pltpu.CompilerParams(vmem_limit_bytes=SMALL_VMEM),
        name="mix_rows",
    )(tile, in_vmem(other), in_vmem(other_hit), in_vmem(own_mixed), taps)


def deinterleave(rows):
    row = lax.broadcasted_iota(jnp.int32, (128, 128), 0)
    col = lax.broadcasted_iota(jnp.int32, (128, 128), 1)
    order = jnp.where(col == 2 * (row % BLOCKS) + row // BLOCKS, 1.0, 0.0).astype(bf16)
    return jnp.dot(order, rows, preferred_element_type=f32).astype(bf16)


def project_own_kernel(tile_ref, own_ref, w_ref, part_ref, rows_s):
    for j in range(PAIRS):
        rows = own_ref[:, :, j * PART : (j + 1) * PART].reshape(128, PART)
        rows_s[j * 128 : (j + 1) * 128, :] = deinterleave(rows)
    first = pl.multiple_of(512 * tile_ref[0], 128)
    for lo in range(0, OUT_DEV, 256):
        weights = w_ref[pl.ds(first, PART), lo : lo + 256]
        part_ref[:, lo : lo + 256] = jnp.dot(rows_s[...], weights, preferred_element_type=f32)


def project_own(tile, own, w_proj):
    smem, vmem = (pl.BlockSpec(memory_space=m) for m in (pltpu.SMEM, pltpu.VMEM))
    return pl.pallas_call(
        project_own_kernel,
        in_specs=[smem, vmem, vmem],
        out_specs=vmem,
        out_shape=pltpu.VMEM((FR_DEV * BLOCKS, OUT_DEV), f32),
        scratch_shapes=[pltpu.VMEM((FR_DEV * BLOCKS, PART), bf16)],
        compiler_params=pltpu.CompilerParams(vmem_limit_bytes=SMALL_VMEM),
        name="project_own_channels",
    )(tile, in_vmem(own), in_vmem(w_proj))


def project_kernel(tile_ref, other_ref, part_ref, w_ref, out_hbm, rows_s, out_s, sems):
    tile = tile_ref[0]
    for j in range(PAIRS):
        cols = pl.ds(pl.multiple_of(j * PART + 128 * (1 - tile), 128), REST)
        rows_s[j * 128 : (j + 1) * 128, :] = deinterleave(other_ref[:, :, cols].reshape(128, REST))
    first = pl.multiple_of(PART * (1 - tile), 128)
    copies = []
    for n, (lo, hi) in enumerate(zip(OUT_CUTS[:-1], OUT_CUTS[1:])):
        for mid in range(lo, hi, 256):
            cols = slice(mid, mid + 256)
            weights = w_ref[pl.ds(first, REST), cols]
            out = jnp.dot(rows_s[...], weights, preferred_element_type=f32) + part_ref[:, cols]
            out_s[:, :, cols] = out.astype(bf16).reshape(FR_DEV, BLOCKS, 256)
        cols = pl.ds(lo, hi - lo)
        copies.append(
            pltpu.make_async_copy(out_s.at[:, :, cols], out_hbm.at[:, :, cols], sems.at[n])
        )
        copies[n].start()
    for copy in copies:
        copy.wait()


def project(tile, other, part, w_proj):
    smem, vmem = (pl.BlockSpec(memory_space=m) for m in (pltpu.SMEM, pltpu.VMEM))
    shape = (FR_DEV, BLOCKS, OUT_DEV)
    return pl.pallas_call(
        project_kernel,
        in_specs=[smem, vmem, vmem, vmem],
        out_specs=pl.BlockSpec(memory_space=pltpu.HBM),
        out_shape=jax.ShapeDtypeStruct(shape, bf16),
        scratch_shapes=[
            pltpu.VMEM((FR_DEV * BLOCKS, REST), bf16),
            pltpu.VMEM(shape, bf16),
            pltpu.SemaphoreType.DMA((len(OUT_CUTS) - 1,)),
        ],
        compiler_params=pltpu.CompilerParams(vmem_limit_bytes=SMALL_VMEM),
        name="project_rows",
    )(tile, in_vmem(other), in_vmem(part), in_vmem(w_proj))


SWAP = [(0, 1), (1, 0)]


def on_device(
    frames_in, norm_gain, norm_bias, w_qkv, w_out, time_taps, w_proj, clip_lengths, frame_slot, block_map
):
    core = jnp.reshape(lax.axis_index("tile"), (1,)).astype(jnp.int32)
    sent = cut_sent(core, frames_in)
    other = lax.ppermute(sent, "tile", SWAP)
    frames_in, _ = lax.optimization_barrier((frames_in, sent))
    own, own_normed, w_qkv, pool = stage(
        core, frames_in, norm_gain, norm_bias, block_map[None], w_qkv
    )
    pooled = encode(
        own, own_normed, other, norm_gain, norm_bias, w_qkv, w_out, pool
    )
    spread = lax.all_to_all(pooled, "frame", split_axis=0, concat_axis=0, tiled=True)
    spread_other = lax.ppermute(spread, "tile", SWAP)
    other_hit, own_mixed = pick(core, clip_lengths, frame_slot[None], spread, time_taps)
    mixed = mix(core, spread_other, other_hit, own_mixed, time_taps)
    home = lax.all_to_all(mixed, "frame", split_axis=0, concat_axis=0, tiled=True)
    home_other = lax.ppermute(home, "tile", SWAP)
    part = project_own(core, home, w_proj)
    return project(core, home_other, part, w_proj)


def solution(mesh):
    in_specs = (P("frame", "tile", None), P(), P(), P(), P(), P(), P(None, "tile"), P(), P(), P())
    return jax.shard_map(
        on_device, mesh=mesh, in_specs=in_specs, out_specs=P("frame", None, "tile"), check_vma=False
    )
```

```python
import math

import jax
import jax.numpy as jnp
from jax import lax
from jax.experimental import pallas as pl
from jax.experimental.pallas import tpu as pltpu
from jax.sharding import PartitionSpec as P

D = 1152
HEADS = 16
HEAD_DIM = 72
PATCH = 256
HALF = 128
BLOCKS = 64
FRAMES = 384
FRAME_DEVS = 64
CLIPS = 6
FR_DEV = 6
SLOT_DEV = 12
SLOTS = 768
PAIRS = 3
PIECES = 9
PART = 640
REST = 512
OUT_CUTS = (0, 512, 1024, 1536, 1792)
OUT_DEV = 1792
NORM_EPS = 1e-6
SCORE_SCALE = math.log2(math.e) / math.sqrt(HEAD_DIM)
STAGE_VMEM = 16 << 20
ENCODE_VMEM = 34 << 20
SMALL_VMEM = 16 << 20

bf16 = jnp.bfloat16
f32 = jnp.float32
NT = (((1,), (1,)), ((), ()))


def head_lanes(head):
    first, last = HEAD_DIM * head, HEAD_DIM * (head + 1) - 1
    return first // 128 * 128, (last // 128 + 1) * 128


def in_vmem(x):
    return pltpu.with_memory_space_constraint(x, pltpu.VMEM)


def in_hbm(x):
    return pltpu.with_memory_space_constraint(x, pltpu.HBM)


def normalise(rows, gain_ref, bias_ref):
    gain, bias = gain_ref[...].reshape(1, D), bias_ref[...].reshape(1, D)
    rows = rows.astype(f32)
    centred = rows - jnp.sum(rows, -1, keepdims=True) * (1.0 / D)
    variance = jnp.sum(centred * centred, -1, keepdims=True) * (1.0 / D)
    return (centred * lax.rsqrt(variance + NORM_EPS) * gain + bias).astype(bf16)


def cut_kernel(tile_ref, frames_hbm, out_ref, sems):
    first = FR_DEV * (1 - tile_ref[0])
    copies = []
    for n in range(2):
        source = frames_hbm.at[pl.ds(first + PAIRS * n, PAIRS)]
        copies.append(
            pltpu.make_async_copy(source, out_ref.at[pl.ds(PAIRS * n, PAIRS)], sems.at[n])
        )
        copies[n].start()
    for copy in copies:
        copy.wait()


def cut_sent(tile, frames_in):
    return pl.pallas_call(
        cut_kernel,
        in_specs=[pl.BlockSpec(memory_space=m) for m in (pltpu.SMEM, pltpu.HBM)],
        out_specs=pl.BlockSpec(memory_space=pltpu.VMEM),
        out_shape=pltpu.VMEM((FR_DEV, HALF, D), bf16),
        scratch_shapes=[pltpu.SemaphoreType.DMA((2,))],
        compiler_params=pltpu.CompilerParams(vmem_limit_bytes=STAGE_VMEM),
        name="cut_sent_half",
    )(tile, in_hbm(frames_in))


def stage_kernel(
    tile_ref, frames_hbm, gain_ref, bias_ref, map_ref, wqkv_hbm,
    own_ref, normed_ref, wqkv_ref, pool_ref, sems,
):
    rows = pl.ds(FR_DEV * tile_ref[0], FR_DEV)
    copies = [pltpu.make_async_copy(frames_hbm.at[rows], own_ref, sems.at[0])]
    step = D // PIECES
    for n in range(PIECES):
        part = pl.ds(n * step, step)
        copies.append(pltpu.make_async_copy(wqkv_hbm.at[part], wqkv_ref.at[part], sems.at[n + 1]))
    for copy in copies:
        copy.start()
    pool_ref[...] = pooling(tile_ref[0], map_ref)
    copies[0].wait()
    for f in range(FR_DEV):
        normed_ref[f] = normalise(own_ref[f], gain_ref, bias_ref)
    for copy in copies[1:]:
        copy.wait()


def stage(tile, frames_in, gain, bias, block_map, w_qkv):
    smem, vmem, hbm = (pl.BlockSpec(memory_space=m) for m in (pltpu.SMEM, pltpu.VMEM, pltpu.HBM))
    return pl.pallas_call(
        stage_kernel,
        in_specs=[smem, hbm, vmem, vmem, vmem, hbm],
        out_specs=[vmem] * 4,
        out_shape=[
            pltpu.VMEM((FR_DEV, HALF, D), bf16),
            pltpu.VMEM((FR_DEV, HALF, D), bf16),
            pltpu.VMEM((D, 3 * D), bf16),
            pltpu.VMEM((2 * BLOCKS, 2 * PATCH), bf16),
        ],
        scratch_shapes=[pltpu.SemaphoreType.DMA((1 + PIECES,))],
        compiler_params=pltpu.CompilerParams(vmem_limit_bytes=STAGE_VMEM),
        name="stage_operands",
    )(tile, in_hbm(frames_in), gain, bias, block_map, in_hbm(w_qkv))


def project_qkv(normed_s, w_ref, qk_s, vt_s):
    starts = list(range(2 * D, 3 * D, 256)) + [0, 1024, 256, 1280, 512, 1536, 768, 1792, 2048]
    for lo in starts:
        hi = min(lo + 256, 3 * D)
        part = jnp.dot(normed_s[...], w_ref[:, lo:hi], preferred_element_type=f32)
        if hi <= 2 * D:
            qk_s[:, lo:hi] = part.astype(bf16)
        else:
            vt_s[lo - 2 * D : hi - 2 * D, :] = part.astype(bf16).T


def attend(qk_s, vt_s, ctx_s):
    lane = lax.broadcasted_iota(jnp.int32, (1, D), 1)
    ones = jnp.ones((16, PATCH), bf16)

    def scores(s, head):
        lo, hi = head_lanes(head)
        start = HEAD_DIM * head
        mine = (lane[:, lo:hi] >= start) & (lane[:, lo:hi] < start + HEAD_DIM)
        rows = slice(s * PATCH, (s + 1) * PATCH)
        keys = qk_s[rows, D + lo : D + hi]
        keys = jnp.where(mine, keys, jnp.zeros_like(keys))
        return lax.dot_general(keys, qk_s[rows, lo:hi], NT, preferred_element_type=f32)

    def weigh(score):
        top = jnp.max(score, 0, keepdims=True)
        return jnp.exp2((score - top) * SCORE_SCALE).astype(bf16)

    def total(s, head, weights):
        skip = 8 * (head % 2)
        first = HEAD_DIM * head - skip
        cols = slice(s * PATCH, (s + 1) * PATCH)
        values = jnp.concatenate([vt_s[first : first + 80, cols], ones], 0)
        summed = jnp.dot(values, weights, preferred_element_type=f32)
        ctx_s[HEAD_DIM * head : HEAD_DIM * (head + 1), cols] = (
            summed[skip : skip + HEAD_DIM] / summed[80:81]
        )

    items = [(s, head) for s in range(2) for head in range(HEADS)]
    score, weights = {}, {}
    for n in range(-6, len(items)):
        if 0 <= n + 3 < len(items):
            weights[n + 3] = weigh(score.pop(n + 3))
        if 0 <= n + 6 < len(items):
            score[n + 6] = scores(*items[n + 6])
        if n >= 0:
            total(*items[n], weights.pop(n))


def pooling(tile, map_ref):
    block = lax.broadcasted_iota(jnp.int32, (BLOCKS, 2 * PATCH), 0)
    col = lax.broadcasted_iota(jnp.int32, (BLOCKS, 2 * PATCH), 1)
    col_block = (col % HALF) // 4 + BLOCKS // 2 * ((col // HALF + tile) % 2)
    row = lax.broadcasted_iota(jnp.int32, (2 * BLOCKS, 1), 0)
    placing = jnp.where(map_ref[...] == row // 2, 1.0, 0.0).astype(bf16)
    member = jnp.where(block == col_block, 0.25, 0.0).astype(bf16)
    member = jnp.dot(placing, member, preferred_element_type=f32)
    frame_of = lax.broadcasted_iota(jnp.int32, (1, 2 * PATCH), 1) // PATCH
    return jnp.where(frame_of == row % 2, member, 0.0).astype(bf16)


def encode_kernel(
    own_ref, own_normed, other_ref, gain_ref, bias_ref, wqkv_ref, wout_hbm, pool_ref, out_ref,
    wout_s, normed_s, qk_s, vt_s, ctx_s, pooled_x, pooled_ctx, sem,
):
    wout_copy = pltpu.make_async_copy(wout_hbm, wout_s, sem)
    wout_copy.start()

    def one_pair(pair, carry):
        for s in range(2):
            frame = 2 * pair + s
            mid = s * PATCH + HALF
            normed_s[s * PATCH : mid, :] = own_normed[frame]
            normed_s[mid : (s + 1) * PATCH, :] = normalise(other_ref[frame], gain_ref, bias_ref)
        project_qkv(normed_s, wqkv_ref, qk_s, vt_s)
        attend(qk_s, vt_s, ctx_s)
        rows = pl.ds(pl.multiple_of(pair * 2 * BLOCKS, 2 * BLOCKS), 2 * BLOCKS)
        pooled = lax.dot_general(
            pool_ref[...], ctx_s[...].astype(bf16), NT, preferred_element_type=f32
        )
        pooled_ctx[rows, :] = pooled.astype(bf16)
        patches = [ref[2 * pair + s] for s in range(2) for ref in (own_ref, other_ref)]
        patches = jnp.concatenate(patches, 0)
        pooled_x[rows, :] = jnp.dot(pool_ref[...], patches, preferred_element_type=f32)
        return carry

    lax.fori_loop(0, PAIRS, one_pair, 0)
    wout_copy.wait()
    for pair in range(PAIRS):
        rows = slice(pair * 2 * BLOCKS, (pair + 1) * 2 * BLOCKS)
        total = jnp.dot(pooled_ctx[rows, :], wout_s[...], preferred_element_type=f32)
        total = (total + pooled_x[rows, :]).astype(bf16)
        out_ref[:, :, pair * D : (pair + 1) * D] = total.reshape(BLOCKS, 2, D)


def encode(own, own_normed, other, gain, bias, w_qkv, w_out, pool):
    vmem, hbm = (pl.BlockSpec(memory_space=m) for m in (pltpu.VMEM, pltpu.HBM))
    return pl.pallas_call(
        encode_kernel,
        in_specs=[vmem] * 6 + [hbm, vmem],
        out_specs=vmem,
        out_shape=pltpu.VMEM((BLOCKS, 2, PAIRS * D), bf16),
        scratch_shapes=[
            pltpu.VMEM((D, D), bf16),
            pltpu.VMEM((2 * PATCH, D), bf16),
            pltpu.VMEM((2 * PATCH, 2 * D), bf16),
            pltpu.VMEM((D, 2 * PATCH), bf16),
            pltpu.VMEM((D, 2 * PATCH), f32),
            pltpu.VMEM((PAIRS * 2 * BLOCKS, D), f32),
            pltpu.VMEM((PAIRS * 2 * BLOCKS, D), bf16),
            pltpu.SemaphoreType.DMA,
        ],
        compiler_params=pltpu.CompilerParams(vmem_limit_bytes=ENCODE_VMEM),
        name="encode_frames",
    )(
        in_vmem(own), in_vmem(own_normed), in_vmem(other), gain, bias,
        in_vmem(w_qkv), in_hbm(w_out), in_vmem(pool),
    )


def own_rows(ref, rows_s, tile):
    for j in range(PAIRS):
        cols = pl.ds(pl.multiple_of(j * D + 512 * tile, 128), PART)
        rows_s[j * 128 : (j + 1) * 128, :] = ref[:, :, cols].reshape(128, PART)


def tap_sum(picked, taps, step):
    total = 0.0
    for tap in range(3):
        first = (PAIRS * step + tap) * 128
        total += taps[tap : tap + 1] * picked[first : first + 128, :]
    return total


def pick_kernel(
    tile_ref, lengths_ref, slots_ref, own_ref, taps_ref, other_hit, mixed_ref,
    rows_s, own_hit, picked_s,
):
    tile = tile_ref[0]
    own_rows(own_ref, rows_s, tile)
    code = slots_ref[...] + 1
    code = jnp.concatenate([code // 16, code % 16] + [jnp.zeros_like(code)] * 6, 0)
    slot = lax.broadcasted_iota(jnp.int32, (SLOTS, SLOTS), 0)
    col = lax.broadcasted_iota(jnp.int32, (1, SLOTS), 1)
    group, place = col // 128, col % 128
    core = (group // PAIRS + tile) % 2
    source = SLOT_DEV * (place // 2) + FR_DEV * core + 2 * (group % PAIRS) + place % 2
    moved = jnp.where(slot == source, 1.0, 0.0).astype(bf16)
    code = jnp.dot(code.astype(f32).astype(bf16), moved, preferred_element_type=f32)
    held = (code[0:1] * 16.0 + code[1:2]).astype(jnp.int32) - 1
    row = lax.broadcasted_iota(jnp.int32, (128, 1), 0)
    for step in range(PAIRS):
        frame = FR_DEV * (row // 2) + 2 * step + row % 2
        first, last = frame < 0, frame + 1 == FRAMES
        start = 0
        for c in range(CLIPS):
            first |= frame == start
            last |= frame + 1 == start
            start += lengths_ref[c]
        wanted = (jnp.where(first, -2, frame - 1), frame, jnp.where(last, -2, frame + 1))
        for tap, want in enumerate(wanted):
            rows = slice((PAIRS * step + tap) * 128, (PAIRS * step + tap + 1) * 128)
            hit = jnp.where(held == want, 1.0, 0.0).astype(bf16)
            own_hit[rows, :] = hit[:, : SLOTS // 2]
            other_hit[rows, :] = hit[:, SLOTS // 2 :]
    picked_s[...] = jnp.dot(own_hit[...], rows_s[...], preferred_element_type=f32)
    taps = taps_ref[:, pl.ds(pl.multiple_of(512 * tile, 128), PART)]
    for step in range(PAIRS):
        mixed_ref[step * 128 : (step + 1) * 128, :] = tap_sum(picked_s, taps, step)


def pick(tile, lengths, slots, own, taps):
    smem, vmem = (pl.BlockSpec(memory_space=m) for m in (pltpu.SMEM, pltpu.VMEM))
    return pl.pallas_call(
        pick_kernel,
        in_specs=[smem, smem, vmem, vmem, vmem],
        out_specs=[vmem, vmem],
        out_shape=[
            pltpu.VMEM((9 * 128, SLOTS // 2), bf16),
            pltpu.VMEM((PAIRS * 128, PART), f32),
        ],
        scratch_shapes=[
            pltpu.VMEM((SLOTS // 2, PART), bf16),
            pltpu.VMEM((9 * 128, SLOTS // 2), bf16),
            pltpu.VMEM((9 * 128, PART), f32),
        ],
        compiler_params=pltpu.CompilerParams(vmem_limit_bytes=SMALL_VMEM),
        name="pick_own_rows",
    )(tile, lengths, slots, in_vmem(own), taps)


def mix_kernel(tile_ref, other_ref, other_hit, own_mixed, taps_ref, out_ref, rows_s, picked_s):
    tile = tile_ref[0]
    own_rows(other_ref, rows_s, tile)
    picked_s[...] = jnp.dot(other_hit[...], rows_s[...], preferred_element_type=f32)
    taps = taps_ref[:, pl.ds(pl.multiple_of(512 * tile, 128), PART)]
    for step in range(PAIRS):
        mixed = own_mixed[step * 128 : (step + 1) * 128, :] + tap_sum(picked_s, taps, step)
        mixed = mixed.astype(bf16).reshape(FRAME_DEVS, 2, PART)
        out_ref[:, :, step * PART : (step + 1) * PART] = mixed


def mix(tile, other, other_hit, own_mixed, taps):
    smem, vmem = (pl.BlockSpec(memory_space=m) for m in (pltpu.SMEM, pltpu.VMEM))
    return pl.pallas_call(
        mix_kernel,
        in_specs=[smem, vmem, vmem, vmem, vmem],
        out_specs=vmem,
        out_shape=pltpu.VMEM((FRAME_DEVS, 2, PAIRS * PART), bf16),
        scratch_shapes=[
            pltpu.VMEM((SLOTS // 2, PART), bf16),
            pltpu.VMEM((9 * 128, PART), f32),
        ],
        compiler_params=pltpu.CompilerParams(vmem_limit_bytes=SMALL_VMEM),
        name="mix_rows",
    )(tile, in_vmem(other), in_vmem(other_hit), in_vmem(own_mixed), taps)


def deinterleave(rows):
    row = lax.broadcasted_iota(jnp.int32, (128, 128), 0)
    col = lax.broadcasted_iota(jnp.int32, (128, 128), 1)
    order = jnp.where(col == 2 * (row % BLOCKS) + row // BLOCKS, 1.0, 0.0).astype(bf16)
    return jnp.dot(order, rows, preferred_element_type=f32).astype(bf16)


def project_own_kernel(tile_ref, own_ref, w_ref, part_ref, rows_s):
    for j in range(PAIRS):
        rows = own_ref[:, :, j * PART : (j + 1) * PART].reshape(128, PART)
        rows_s[j * 128 : (j + 1) * 128, :] = deinterleave(rows)
    first = pl.multiple_of(512 * tile_ref[0], 128)
    for lo in range(0, OUT_DEV, 256):
        weights = w_ref[pl.ds(first, PART), lo : lo + 256]
        part_ref[:, lo : lo + 256] = jnp.dot(rows_s[...], weights, preferred_element_type=f32)


def project_own(tile, own, w_proj):
    smem, vmem = (pl.BlockSpec(memory_space=m) for m in (pltpu.SMEM, pltpu.VMEM))
    return pl.pallas_call(
        project_own_kernel,
        in_specs=[smem, vmem, vmem],
        out_specs=vmem,
        out_shape=pltpu.VMEM((FR_DEV * BLOCKS, OUT_DEV), f32),
        scratch_shapes=[pltpu.VMEM((FR_DEV * BLOCKS, PART), bf16)],
        compiler_params=pltpu.CompilerParams(vmem_limit_bytes=SMALL_VMEM),
        name="project_own_channels",
    )(tile, in_vmem(own), in_vmem(w_proj))


def project_kernel(tile_ref, other_ref, part_ref, w_ref, out_hbm, rows_s, out_s, sems):
    tile = tile_ref[0]
    for j in range(PAIRS):
        cols = pl.ds(pl.multiple_of(j * PART + 128 * (1 - tile), 128), REST)
        rows_s[j * 128 : (j + 1) * 128, :] = deinterleave(other_ref[:, :, cols].reshape(128, REST))
    first = pl.multiple_of(PART * (1 - tile), 128)
    copies = []
    for n, (lo, hi) in enumerate(zip(OUT_CUTS[:-1], OUT_CUTS[1:])):
        for mid in range(lo, hi, 256):
            cols = slice(mid, mid + 256)
            weights = w_ref[pl.ds(first, REST), cols]
            out = jnp.dot(rows_s[...], weights, preferred_element_type=f32) + part_ref[:, cols]
            out_s[:, :, cols] = out.astype(bf16).reshape(FR_DEV, BLOCKS, 256)
        cols = pl.ds(lo, hi - lo)
        copies.append(
            pltpu.make_async_copy(out_s.at[:, :, cols], out_hbm.at[:, :, cols], sems.at[n])
        )
        copies[n].start()
    for copy in copies:
        copy.wait()


def project(tile, other, part, w_proj):
    smem, vmem = (pl.BlockSpec(memory_space=m) for m in (pltpu.SMEM, pltpu.VMEM))
    shape = (FR_DEV, BLOCKS, OUT_DEV)
    return pl.pallas_call(
        project_kernel,
        in_specs=[smem, vmem, vmem, vmem],
        out_specs=pl.BlockSpec(memory_space=pltpu.HBM),
        out_shape=jax.ShapeDtypeStruct(shape, bf16),
        scratch_shapes=[
            pltpu.VMEM((FR_DEV * BLOCKS, REST), bf16),
            pltpu.VMEM(shape, bf16),
            pltpu.SemaphoreType.DMA((len(OUT_CUTS) - 1,)),
        ],
        compiler_params=pltpu.CompilerParams(vmem_limit_bytes=SMALL_VMEM),
        name="project_rows",
    )(tile, in_vmem(other), in_vmem(part), in_vmem(w_proj))


SWAP = [(0, 1), (1, 0)]


def on_device(
    frames_in, norm_gain, norm_bias, w_qkv, w_out, time_taps, w_proj, clip_lengths, frame_slot, block_map
):
    core = jnp.reshape(lax.axis_index("tile"), (1,)).astype(jnp.int32)
    sent = cut_sent(core, frames_in)
    other = lax.ppermute(sent, "tile", SWAP)
    frames_in, _ = lax.optimization_barrier((frames_in, sent))
    own, own_normed, w_qkv, pool = stage(
        core, frames_in, norm_gain, norm_bias, block_map[None], w_qkv
    )
    pooled = encode(
        own, own_normed, other, norm_gain, norm_bias, w_qkv, w_out, pool
    )
    spread = lax.all_to_all(pooled, "frame", split_axis=0, concat_axis=0, tiled=True)
    spread_other = lax.ppermute(spread, "tile", SWAP)
    other_hit, own_mixed = pick(core, clip_lengths, frame_slot[None], spread, time_taps)
    mixed = mix(core, spread_other, other_hit, own_mixed, time_taps)
    home = lax.all_to_all(mixed, "frame", split_axis=0, concat_axis=0, tiled=True)
    home_other = lax.ppermute(home, "tile", SWAP)
    part = project_own(core, home, w_proj)
    return project(core, home_other, part, w_proj)


def solution(mesh):
    in_specs = (P("frame", "tile", None), P(), P(), P(), P(), P(), P(None, "tile"), P(), P(), P())
    return jax.shard_map(
        on_device, mesh=mesh, in_specs=in_specs, out_specs=P("frame", None, "tile"), check_vma=False
    )
```
